512 devices in a mesh: snp: 32 (over y, x, core), samp: 16 (over z).
Axes of the slice: x: 4, y: 4, z: 16, core: 2. Of those that a mesh axis runs over, the one named last changes fastest.
Arguments:
- dosages: bfloat16 [24576, 16384], P('samp', 'snp'), may hold values from 0 to 2
- observed: int32 [24576, 16384], P('samp', 'snp'), may hold values from 0 to 1, as said below
Outputs:
- band_gram: float32 [16384, 1536], P(('snp', 'samp'))
The draws below stay inside these ranges and needn't reach their ends.
Inputs may be any that keep to these rules, and one draw needn't show every extreme that they name: Some SNP columns are missing in every sample, so their count of observed samples is 0.
All inputs are finite; a program needn't handle non-finite values.
Results may differ from the reference program's by a relative error of at most 0.00095.
Values may be sent and summed in bfloat16 or wider, within the bound.
A program may use at most 64 MiB of HBM per device.

```python
import jax
import jax.numpy as jnp
from jax import lax

BLOCK = 512
SAMPLES = 24576
MARKERS = 16384


def draw_observed(key, part):
    key = jax.random.fold_in(key, 7)
    mask_key, column_key = jax.random.split(key)
    base = (jax.random.randint(mask_key, (SAMPLES, MARKERS), 0, 10) < 9).astype(jnp.int32)
    columns = jax.random.randint(column_key, (4,), 0, MARKERS)
    positions = jnp.arange(MARKERS, dtype=jnp.int32)
    missing = jnp.any(positions[None, :] == columns[:, None], axis=0)
    return jnp.where(missing[None, :], 0, base).astype(jnp.int32)


def shard_levels(stream_key, shape, pieces, least, top_value):
    loudness = 1.0
    for dim, blocks in pieces:
        heights = jax.random.uniform(jax.random.fold_in(jax.random.fold_in(stream_key, 6), dim), (blocks,), jnp.float32, least / len(pieces), top_value / len(pieces))
        loudness = loudness * jnp.repeat(jnp.exp(heights), shape[dim] // blocks).reshape((-1,) + (1,) * (len(shape) - 1 - dim))
    return loudness


def setup_inputs(seed: int = 0) -> dict:
    key_of = jax.random.split(jax.random.key(seed), 3)
    return {
        "dosages": jnp.clip(2.0 * jax.random.uniform(key_of[0], (SAMPLES, MARKERS), jnp.float32) ** shard_levels(key_of[0], (SAMPLES, MARKERS), ((0, 16), (1, 32)), -0.2, 0.2), 0.0, 2.0).astype(jnp.bfloat16),
        "observed": draw_observed(jax.random.fold_in(key_of[2], 71), 0),
    }


def reference(dosages, observed):
    mask_f = observed.astype(jnp.float32)
    values = dosages.astype(jnp.float32)
    count = jnp.maximum(lax.optimization_barrier(jnp.sum(mask_f, axis=0)), 1.0)
    mean = lax.optimization_barrier(jnp.sum(mask_f * values, axis=0)) / count
    var = lax.optimization_barrier(jnp.sum(mask_f * values * values, axis=0)) / count - mean * mean
    standard = (mask_f * (values - mean) * lax.rsqrt(var + 1e-05)).astype(jnp.bfloat16)
    padded = jnp.concatenate([standard, jnp.zeros((standard.shape[0], 2 * BLOCK), jnp.bfloat16)], axis=1)
    blocks = standard.shape[1] // BLOCK

    def one_block(index):
        start = index * BLOCK
        own = lax.dynamic_slice_in_dim(padded, start, BLOCK, 1)
        wide = lax.dynamic_slice_in_dim(padded, start, 3 * BLOCK, 1)
        gram = lax.dot_general(own, wide, (((0,), (0,)), ((), ())), preferred_element_type=jnp.float32)
        return gram / jnp.float32(SAMPLES)
    result = lax.map(one_block, jnp.arange(blocks, dtype=jnp.int32))
    return result.reshape(MARKERS, 3 * BLOCK)
```

```python
import functools
import math

import jax
import jax.numpy as jnp
from jax import lax
from jax.experimental import pallas as pl
from jax.experimental.pallas import tpu as pltpu
from jax.sharding import PartitionSpec as P

MESH = pl.DeviceIdType.MESH
F32 = jnp.float32
BF16 = jnp.bfloat16

STEPS = 1650.0
FINE = 4096.0


def encode(x):
    q = jnp.minimum(STEPS * jnp.log(1.0 + FINE * jnp.abs(x)) + 0.5, 32767.0).astype(
        jnp.int32
    )
    return jnp.where(x < 0.0, -q, q).astype(jnp.int16)


def decode(q):
    f = q.astype(jnp.int32).astype(F32)
    a = (jnp.exp(jnp.abs(f) * (1.0 / STEPS)) - 1.0) * (1.0 / FINE)
    return jnp.where(f < 0.0, -a, a)


def gram(left, right):
    return lax.dot_general(
        left, right, (((0,), (0,)), ((), ())), preferred_element_type=F32
    )


class Chain:
    def __init__(self, groups, stride, part, stage, slots, send, recv, device):
        self.groups, self.stride = groups, stride
        self.reach = (groups // 2, groups - 1 - groups // 2)
        self.part, self.stage, self.slots = part, stage, slots
        self.send, self.recv, self.device = send, recv, device

    def hop(self, way, offset, source, number):
        stride, reach = self.stride, self.reach[way]
        length = min(stride, offset)
        slot = offset - stride if offset > stride else reach - stride + offset
        sign = 1 if way == 0 else -1
        return pltpu.make_async_remote_copy(
            src_ref=source,
            dst_ref=self.slots.at[way, slot - 1],
            send_sem=self.send.at[way, number],
            recv_sem=self.recv.at[way, slot - 1],
            device_id=self.device(sign * length),
            device_id_type=MESH,
        )

    def arrival(self, way, slot):
        ref = self.slots.at[way, slot - 1]
        return pltpu.make_async_copy(ref, ref, self.recv.at[way, slot - 1])

    def own(self, way, offset):
        me = lax.axis_index("samp")
        sign = 1 if way == 0 else -1
        return lax.rem(me + sign * offset + self.groups, self.groups)

    def source(self, way, offset):
        reach, stride = self.reach[way], self.stride
        if offset + stride > reach:
            return self.stage.at[way, reach - offset]
        return self.slots.at[way, offset - 1]

    def visit(self, way, offset):
        reach, stride = self.reach[way], self.stride
        ref = self.source(way, offset)
        total = self.part[self.own(way, offset)]
        if offset + stride <= reach:
            self.arrival(way, offset).wait()
            total = total + decode(ref[...])
        ref[...] = encode(total)
        self.hop(way, offset, ref, offset - 1).start()

    def start(self):
        for way in (0, 1):
            for offset in range(self.reach[way], self.reach[way] - self.stride, -1):
                self.visit(way, offset)

    def levels(self):
        top = self.reach[0] - self.stride
        steps = []
        while top > 0:
            steps.append(
                [
                    (way, offset)
                    for offset in range(top, max(top - self.stride, 0), -1)
                    for way in (0, 1)
                    if offset + self.stride <= self.reach[way]
                ]
            )
            top -= self.stride
        return steps

    def finish(self):
        total = self.part[lax.axis_index("samp")]
        for way in (0, 1):
            for near in range(1, self.stride + 1):
                slot = self.reach[way] - self.stride + near
                self.arrival(way, slot).wait()
                total = total + decode(self.slots[way, slot - 1])
        return total

    def drain(self):
        for way in (0, 1):
            for offset in range(1, self.reach[way] + 1):
                self.hop(way, offset, self.source(way, offset), offset - 1).wait_send()


def band_kernel(
    groups,
    chips,
    dosages,
    observed,
    out,
    dose_v,
    seen_v,
    stats,
    blocks,
    ordered,
    ahead,
    behind,
    part_e,
    part_l,
    stage_e,
    stage_l,
    slots_e,
    slots_l,
    give_e,
    give_l,
    give_p,
    take_e,
    take_l,
    take_p,
    load_sem,
    stat_send,
    stat_recv,
    core_send,
    core_recv,
    x_send,
    x_recv,
    e_send,
    e_recv,
    l_send,
    l_recv,
    f_send,
    f_recv,
):
    snp, me = lax.axis_index("snp"), lax.axis_index("samp")
    core = lax.rem(snp, 2)
    chip = lax.div(snp, 2)
    rows, width = dose_v.shape
    samples = rows * groups
    count_snp = 2 * chips

    def along(distance):
        return (snp, lax.rem(me + distance + groups, groups))

    other = (snp + 1 - 2 * core, me)
    before = (lax.rem(snp + count_snp - 2, count_snp), me)
    after = (lax.rem(snp + 2, count_snp), me)
    cross = (lax.rem(snp + count_snp + 2 * core - 1, count_snp), me)
    before_b = (lax.rem(2 * chip + count_snp - 1, count_snp), me)

    def remote(src, dst, send, recv, device):
        return pltpu.make_async_remote_copy(
            src_ref=src,
            dst_ref=dst,
            send_sem=send,
            recv_sem=recv,
            device_id=device,
            device_id_type=MESH,
        )

    pieces = load_sem.shape[1]
    high = rows // pieces

    def load(piece):
        span = pl.ds(piece * high, high)
        return (
            pltpu.make_async_copy(
                dosages.at[span], dose_v.at[span], load_sem.at[0, piece]
            ),
            pltpu.make_async_copy(
                observed.at[span], seen_v.at[span], load_sem.at[1, piece]
            ),
        )

    for piece in range(pieces):
        for copy in load(piece):
            copy.start()

    barrier = pltpu.get_barrier_semaphore()
    peers = [along(d) for d in range(1, groups)] + [other, before, after, cross]
    for peer in peers:
        pl.semaphore_signal(barrier, inc=1, device_id=peer, device_id_type=MESH)

    def add_rows(step, carry):
        span = pl.ds(pl.multiple_of(step * 32, 32), 32)
        v = dose_v[span].astype(F32)
        m = seen_v[span].astype(F32)
        mv = m * v
        sums = []
        for acc, term in zip(carry, (m, mv, mv * v)):
            sums.append(acc + jnp.sum(term.reshape(4, 8, width), axis=0))
        return tuple(sums)

    carry = tuple(jnp.zeros((8, width), F32) for _ in range(3))
    for piece in range(pieces):
        for copy in load(piece):
            copy.wait()
        carry = lax.fori_loop(
            piece * high // 32, (piece + 1) * high // 32, add_rows, carry
        )
    lanes = width // 128
    stats[me] = jnp.zeros(stats.shape[1:], F32)
    for kind, acc in enumerate(carry):
        line = jnp.sum(acc, axis=0, keepdims=True)
        for lane in range(lanes):
            row = kind * lanes + lane
            stats[me, row : row + 1, :] = line[:, lane * 128 : lane * 128 + 128]

    pl.semaphore_wait(barrier, len(peers))

    half = groups // 2
    order = [half] + [sign * d for d in range(half - 1, 0, -1) for sign in (1, -1)]
    posts = []
    for number, distance in enumerate(order):
        posts.append(
            remote(
                stats.at[me],
                stats.at[me],
                stat_send.at[number],
                stat_recv.at[lax.rem(distance + groups, groups)],
                along(distance),
            )
        )
        posts[-1].start()
    for distance in range(1, groups):
        origin = lax.rem(me - distance + groups, groups)
        ref = stats.at[origin]
        pltpu.make_async_copy(ref, ref, stat_recv.at[distance]).wait()
    total = stats[0]
    for group in range(1, groups):
        total = total + stats[group]
    count = jnp.maximum(total[0:lanes], 1.0)
    mean = total[lanes : 2 * lanes] / count
    var = total[2 * lanes : 3 * lanes] / count - mean * mean
    rate = lax.rsqrt(var + 1e-05)
    mean_line = jnp.concatenate([mean[i : i + 1] for i in range(lanes)], axis=1)
    rate_line = jnp.concatenate([rate[i : i + 1] for i in range(lanes)], axis=1)

    def standardize(step, carry):
        span = pl.ds(pl.multiple_of(step * 32, 32), 32)
        v = dose_v[span].astype(F32)
        m = seen_v[span].astype(F32)
        blocks[core, span, :] = (m * (v - mean_line) * rate_line).astype(BF16)
        return carry

    lax.fori_loop(0, rows // 32, standardize, 0)

    swap = remote(
        blocks.at[core], blocks.at[core], core_send.at[0], core_recv.at[0], other
    )
    swap.start()

    def ahead_copy(chunk):
        cols = pl.ds(pl.multiple_of(core * 256 + chunk * 128, 128), 128)
        return remote(
            blocks.at[0, :, cols],
            ahead.at[chunk],
            x_send.at[0, chunk],
            x_recv.at[0, chunk],
            before,
        )

    def behind_copy(chunk):
        return remote(
            ordered.at[chunk],
            behind.at[chunk],
            x_send.at[1, chunk],
            x_recv.at[1, chunk],
            after,
        )

    def send_ahead():
        for chunk in range(2):
            ahead_copy(chunk).start()

    def send_behind():
        for chunk in range(2):
            line = lax.broadcasted_iota(jnp.int32, (width, 128), 0)
            col = lax.broadcasted_iota(jnp.int32, (width, 128), 1)
            from_row = 32 * (col // 8) + 16 * core + 8 * chunk + lax.rem(col, 8)
            pick = jnp.where(line == from_row, 1.0, 0.0).astype(BF16)
            ordered[chunk] = jnp.dot(
                blocks[1], pick, preferred_element_type=F32
            ).astype(BF16)
            behind_copy(chunk).start()

    pl.when(core == 0)(send_ahead)
    pl.when(core == 1)(send_behind)

    early = Chain(groups, 1, part_e, stage_e, slots_e, e_send, e_recv, along)
    late = [
        Chain(
            groups,
            2,
            part_l.at[chunk],
            stage_l.at[chunk],
            slots_l.at[chunk],
            l_send.at[chunk],
            l_recv.at[chunk],
            along,
        )
        for chunk in range(2)
    ]

    for strip in range(4):
        cols = slice(strip * 128, strip * 128 + 128)
        product = gram(blocks[core, :, cols], blocks[core])
        part_e[strip * 4 : strip * 4 + 4, :, 0:512] = product.reshape(4, 32, 512)

    swap.wait()
    pl.when(core == 1)(send_ahead)
    pl.when(core == 0)(send_behind)

    half_cols = pl.ds(pl.multiple_of(core * 256, 256), 256)
    product = gram(blocks[0], blocks[1, :, half_cols])
    part_e[:, :, 512:768] = product.reshape(16, 32, 256)

    early.start()

    def late_gram(chunk):
        ahead_copy(chunk).wait()
        behind_copy(chunk).wait()
        part = part_l.at[chunk]
        for block in range(2):
            product = gram(blocks[block], ahead[chunk])
            part[:, :, block * 128 : block * 128 + 128] = product.reshape(16, 32, 128)
        product = gram(behind[chunk], blocks[1])
        for piece in range(4):
            cols = slice(piece * 128, piece * 128 + 128)
            part[:, piece * 8 : piece * 8 + 8, 256:384] = product[:, cols].reshape(
                16, 8, 128
            )
        late[chunk].start()

    scale = 1.0 / samples
    last = chip == chips - 1

    def level(chain, number):
        for way, offset in chain.levels()[number]:
            chain.visit(way, offset)

    for number in range(3):
        level(early, number)
    late_gram(0)
    for number in range(3, 5):
        level(early, number)
    level(late[0], 0)
    late_gram(1)
    for number in range(5, 7):
        level(early, number)
        level(late[0], number - 4)
    level(late[1], 0)

    total = early.finish() * scale
    out[:, 0:512] = total[:, 0:512]
    give_e[...] = total[:, 512:768]

    def early_copy():
        return remote(give_e, take_e, f_send.at[0], f_recv.at[0], other)

    pl.when(core == 1)(lambda: early_copy().start())

    def put_early():
        out[:, 512:768] = give_e[...]

    pl.when(core == 0)(put_early)

    def late_copy(chunk):
        return remote(
            give_l.at[chunk],
            take_l.at[chunk],
            f_send.at[1 + chunk],
            f_recv.at[1 + chunk],
            other,
        )

    def back_copy(chunk):
        return remote(
            give_p.at[chunk],
            take_p.at[core, chunk],
            f_send.at[3 + chunk],
            f_recv.at[3 + 2 * core + chunk],
            before_b,
        )

    def late_end(chunk):
        total = late[chunk].finish() * scale
        give_p[chunk] = total[:, 256:384]
        back_copy(chunk).start()
        first = jnp.where(last, 0.0, total[:, 0:128])
        second = jnp.where(last, 0.0, total[:, 128:256])
        give_l[chunk] = jnp.where(core == 0, second, first)
        late_copy(chunk).start()

        def first_core():
            out[:, 1024 + 128 * chunk : 1152 + 128 * chunk] = first

        def second_core():
            out[:, 768 + 128 * chunk : 896 + 128 * chunk] = second

        pl.when(core == 0)(first_core)
        pl.when(core == 1)(second_core)

    late_end(0)
    for number in range(1, 3):
        level(late[1], number)
    late_end(1)

    def arrived(ref, sem):
        pltpu.make_async_copy(ref, ref, sem).wait()

    def first_core_end():
        arrived(take_e, f_recv.at[0])
        out[:, 768:1024] = take_e[...]
        for chunk in range(2):
            arrived(take_l.at[chunk], f_recv.at[1 + chunk])
            out[:, 1280 + 128 * chunk : 1408 + 128 * chunk] = take_l[chunk]

    def second_core_end():
        for chunk in range(2):
            arrived(take_l.at[chunk], f_recv.at[1 + chunk])
            out[:, 512 + 128 * chunk : 640 + 128 * chunk] = take_l[chunk]
        for side in range(2):
            for chunk in range(2):
                ref = take_p.at[side, chunk]
                arrived(ref, f_recv.at[3 + 2 * side + chunk])
                value = jnp.where(last, 0.0, ref[...])
                for piece in range(4):
                    out[
                        16 * side + 8 * chunk : 16 * side + 8 * chunk + 8,
                        1024 + 128 * piece : 1152 + 128 * piece,
                    ] = value[piece * 8 : piece * 8 + 8]

    pl.when(core == 0)(first_core_end)
    pl.when(core == 1)(second_core_end)

    for post in posts:
        post.wait_send()
    early.drain()
    for chunk in range(2):
        late[chunk].drain()
        late_copy(chunk).wait_send()
        back_copy(chunk).wait_send()
    pl.when(core == 1)(lambda: early_copy().wait_send())


def solution(mesh):
    groups, snps = mesh.shape["samp"], mesh.shape["snp"]

    def local(dosages, observed):
        rows, width = dosages.shape
        vmem = pltpu.VMEM
        dma = pltpu.SemaphoreType.DMA
        return pl.pallas_call(
            functools.partial(band_kernel, groups, snps // 2),
            out_shape=jax.ShapeDtypeStruct((width // groups, 3 * width), F32),
            in_specs=[pl.BlockSpec(memory_space=pl.ANY)] * 2,
            out_specs=pl.BlockSpec(memory_space=pltpu.VMEM),
            scratch_shapes=[
                vmem((rows, width), BF16),
                vmem((rows, width), jnp.int32),
                vmem((groups, 16, 128), F32),
                vmem((2, rows, width), BF16),
                vmem((2, rows, 128), BF16),
                vmem((2, rows, 128), BF16),
                vmem((2, rows, 128), BF16),
                vmem((groups, 32, 768), F32),
                vmem((2, groups, 32, 384), F32),
                vmem((2, 1, 32, 768), jnp.int16),
                vmem((2, 2, 2, 32, 384), jnp.int16),
                vmem((2, 8, 32, 768), jnp.int16),
                vmem((2, 2, 8, 32, 384), jnp.int16),
                vmem((32, 256), F32),
                vmem((2, 32, 128), F32),
                vmem((2, 32, 128), F32),
                vmem((32, 256), F32),
                vmem((2, 32, 128), F32),
                vmem((2, 2, 32, 128), F32),
                dma((2, 6)),
                dma((groups,)),
                dma((groups,)),
                dma((1,)),
                dma((1,)),
                dma((2, 2)),
                dma((2, 2)),
                dma((2, 8)),
                dma((2, 8)),
                dma((2, 2, 8)),
                dma((2, 2, 8)),
                dma((5,)),
                dma((7,)),
            ],
            compiler_params=pltpu.CompilerParams(
                collective_id=0,
                has_side_effects=True,
                vmem_limit_bytes=56 * 2**20,
            ),
            cost_estimate=pl.CostEstimate(
                flops=2 * 3 * rows * width * width,
                bytes_accessed=6 * rows * width,
                transcendentals=0,
            ),
            name="band",
        )(dosages, observed)

    return jax.shard_map(
        local,
        mesh=mesh,
        in_specs=(P("samp", "snp"), P("samp", "snp")),
        out_specs=P(("snp", "samp"), None),
        check_vma=False,
    )
```

```python
import functools
import math

import jax
import jax.numpy as jnp
from jax import lax
from jax.experimental import pallas as pl
from jax.experimental.pallas import tpu as pltpu
from jax.sharding import PartitionSpec as P

MESH = pl.DeviceIdType.MESH
F32 = jnp.float32
BF16 = jnp.bfloat16

STEPS = 1650.0
FINE = 4096.0


STRIDES = (1, 1, 1, 1, 1, 2)
ORDER = (((0, 0), (0, 1), (0, 2), (0, 3), (0, 4), (0, 5), (0, 6), (0, 7), (0, 8),), ((0, 0), (0, 1), (1, 0), (2, 0), (3, 0), (1, 1), (0, 2), (2, 1), (4, 0), (3, 1), (1, 2), (0, 3), (2, 2), (4, 1), (3, 2), (1, 3), (5, 0), (4, 2), (2, 3), (0, 4), (3, 3), (1, 4), (4, 3), (2, 4), (0, 5), (3, 4), (5, 1), (1, 5), (4, 4), (2, 5), (0, 6), (3, 5), (1, 6), (4, 5), (2, 6), (5, 2), (0, 7), (3, 6), (1, 7), (4, 6), (2, 7), (0, 8), (3, 7), (5, 3), (1, 8), (4, 7), (2, 8), (3, 8), (5, 4), (4, 8),))


def encode(x):
    q = jnp.minimum(STEPS * jnp.log(1.0 + FINE * jnp.abs(x)) + 0.5, 32767.0).astype(
        jnp.int32
    )
    return jnp.where(x < 0.0, -q, q).astype(jnp.int16)


def decode(q):
    f = q.astype(jnp.int32).astype(F32)
    a = (jnp.exp(jnp.abs(f) * (1.0 / STEPS)) - 1.0) * (1.0 / FINE)
    return jnp.where(f < 0.0, -a, a)


def gram(left, right):
    return lax.dot_general(
        left, right, (((0,), (0,)), ((), ())), preferred_element_type=F32
    )


class Chain:
    def __init__(self, groups, stride, part, stage, slots, send, recv, device):
        self.groups = groups
        self.reach = (groups // 2, groups - 1 - groups // 2)
        self.stride = tuple(min(stride, reach) for reach in self.reach)
        self.part, self.stage, self.slots = part, stage, slots
        self.send, self.recv, self.device = send, recv, device

    def hop(self, way, offset, source, number):
        stride, reach = self.stride[way], self.reach[way]
        length = min(stride, offset)
        slot = offset - stride if offset > stride else reach - stride + offset
        sign = 1 if way == 0 else -1
        return pltpu.make_async_remote_copy(
            src_ref=source,
            dst_ref=self.slots.at[way, slot - 1],
            send_sem=self.send.at[way, number],
            recv_sem=self.recv.at[way, slot - 1],
            device_id=self.device(sign * length),
            device_id_type=MESH,
        )

    def arrival(self, way, slot):
        ref = self.slots.at[way, slot - 1]
        return pltpu.make_async_copy(ref, ref, self.recv.at[way, slot - 1])

    def own(self, way, offset):
        me = lax.axis_index("samp")
        sign = 1 if way == 0 else -1
        return lax.rem(me + sign * offset + self.groups, self.groups)

    def source(self, way, offset):
        reach, stride = self.reach[way], self.stride[way]
        if offset + stride > reach:
            return self.stage.at[way, reach - offset]
        return self.slots.at[way, offset - 1]

    def visit(self, way, offset):
        reach, stride = self.reach[way], self.stride[way]
        ref = self.source(way, offset)
        total = self.part[self.own(way, offset)]
        if offset + stride <= reach:
            self.arrival(way, offset).wait()
            total = total + decode(ref[...])
        ref[...] = encode(total)
        self.hop(way, offset, ref, offset - 1).start()

    def levels(self):
        steps = []
        for way in (0, 1):
            for place, offset in enumerate(range(self.reach[way], 0, -1)):
                number = place // self.stride[way]
                if number == len(steps):
                    steps.append([])
                steps[number].append((place, way, offset))
        return [[visit[1:] for visit in sorted(step)] for step in steps]

    def finish(self):
        total = self.part[lax.axis_index("samp")]
        for near in range(1, max(self.stride) + 1):
            for way in (0, 1):
                if near > self.stride[way]:
                    continue
                slot = self.reach[way] - self.stride[way] + near
                self.arrival(way, slot).wait()
                total = total + decode(self.slots[way, slot - 1])
        return total

    def drain(self):
        for way in (0, 1):
            for offset in range(1, self.reach[way] + 1):
                self.hop(way, offset, self.source(way, offset), offset - 1).wait_send()


def band_kernel(
    groups,
    chips,
    dosages,
    observed,
    out,
    dose_v,
    seen_v,
    stats,
    blocks,
    picks,
    ordered,
    ahead,
    behind,
    raw_ours,
    raw_ahead,
    raw_behind,
    line_ours,
    line_ahead,
    line_behind,
    part_e,
    part_l,
    stage_e,
    stage_l,
    slots_e,
    slots_l,
    give_e,
    give_l,
    give_p,
    take_e,
    take_l,
    take_p,
    load_sem,
    stat_send,
    stat_recv,
    core_send,
    core_recv,
    x_send,
    x_recv,
    r_send,
    r_recv,
    e_send,
    e_recv,
    l_send,
    l_recv,
    f_send,
    f_recv,
):
    snp, me = lax.axis_index("snp"), lax.axis_index("samp")
    core = lax.rem(snp, 2)
    chip = lax.div(snp, 2)
    rows, width = dose_v.shape
    samples = rows * groups
    count_snp = 2 * chips

    def along(distance):
        return (snp, lax.rem(me + distance + groups, groups))

    other = (snp + 1 - 2 * core, me)
    before_b = (lax.rem(2 * chip + count_snp - 1, count_snp), me)
    after_b = (lax.rem(2 * chip + 3, count_snp), me)
    after_a = (lax.rem(2 * chip + 2, count_snp), me)

    def remote(src, dst, send, recv, device):
        return pltpu.make_async_remote_copy(
            src_ref=src,
            dst_ref=dst,
            send_sem=send,
            recv_sem=recv,
            device_id=device,
            device_id_type=MESH,
        )

    pieces = load_sem.shape[1]
    high = rows // pieces

    def load(piece):
        span = pl.ds(piece * high, high)
        return (
            pltpu.make_async_copy(
                dosages.at[span], dose_v.at[span], load_sem.at[0, piece]
            ),
            pltpu.make_async_copy(
                observed.at[span], seen_v.at[span], load_sem.at[1, piece]
            ),
        )

    for piece in range(pieces):
        for copy in load(piece):
            copy.start()

    def make_picks():
        line = lax.broadcasted_iota(jnp.int32, (width, width), 0)
        col = lax.broadcasted_iota(jnp.int32, (width, width), 1)
        from_row = 32 * ((col >> 3) & 15) + 8 * (col >> 7) + (col & 7)
        picks[...] = jnp.where(line == from_row, 1.0, 0.0).astype(BF16)

    barrier = pltpu.get_barrier_semaphore()

    def greet(peers):
        for peer in peers:
            pl.semaphore_signal(barrier, inc=1, device_id=peer, device_id_type=MESH)

    greet([along(d) for d in range(1, groups)] + [other, before_b])
    pl.when(core == 1)(lambda: greet([after_a, after_b]))

    def add_rows(step, carry):
        span = pl.ds(pl.multiple_of(step * 32, 32), 32)
        v = dose_v[span].astype(F32)
        m = seen_v[span].astype(F32)
        mv = m * v
        sums = []
        for acc, term in zip(carry, (m, mv, mv * v)):
            sums.append(acc + jnp.sum(term.reshape(4, 8, width), axis=0))
        return tuple(sums)

    carry = tuple(jnp.zeros((8, width), F32) for _ in range(3))
    for piece in range(pieces):
        for copy in load(piece):
            copy.wait()
        carry = lax.fori_loop(
            piece * high // 32, (piece + 1) * high // 32, add_rows, carry
        )
    lanes = width // 128
    stats[me] = jnp.zeros(stats.shape[1:], F32)
    for kind, acc in enumerate(carry):
        line = jnp.sum(acc, axis=0, keepdims=True)
        for lane in range(lanes):
            row = kind * lanes + lane
            stats[me, row : row + 1, :] = line[:, lane * 128 : lane * 128 + 128]

    def raw_first():
        raw_ours[0] = dose_v[:, 0:128]
        raw_ours[1] = seen_v[:, 0:128].astype(F32).astype(BF16)

    def raw_second():
        make_picks()
        pick = picks[:, 0:128]
        raw_ours[0] = jnp.dot(
            dose_v[...], pick, preferred_element_type=F32
        ).astype(BF16)
        raw_ours[1] = jnp.dot(
            seen_v[...].astype(F32).astype(BF16), pick, preferred_element_type=F32
        ).astype(BF16)

    def raw_copy(side, number):
        source = line_ours if number == 2 else raw_ours.at[number]
        landing = (raw_ahead, raw_behind)[side]
        line = (line_ahead, line_behind)[side]
        return remote(
            source,
            line if number == 2 else landing.at[number],
            r_send.at[side, number],
            r_recv.at[side, number],
            (before_b, after_b)[side],
        )

    with jax.named_scope("raw"):
        pl.when(core == 0)(raw_first)
        pl.when(core == 1)(raw_second)
    with jax.named_scope("entry_wait"):
        pl.semaphore_wait(barrier, groups + 1 + 2 * core)

    half = groups // 2
    order = [half] + [sign * d for d in range(half - 1, 0, -1) for sign in (1, -1)]
    posts = []
    for number, distance in enumerate(order):
        posts.append(
            remote(
                stats.at[me],
                stats.at[me],
                stat_send.at[number],
                stat_recv.at[lax.rem(distance + groups, groups)],
                along(distance),
            )
        )
        posts[-1].start()

    def raw_start(side):
        for number in range(2):
            raw_copy(side, number).start()

    pl.when(core == 0)(lambda: raw_start(0))
    pl.when(core == 1)(lambda: raw_start(1))
    with jax.named_scope("stats_wait"):
        for distance in range(1, groups):
            origin = lax.rem(me - distance + groups, groups)
            ref = stats.at[origin]
            pltpu.make_async_copy(ref, ref, stat_recv.at[distance]).wait()
    total = stats[0]
    for group in range(1, groups):
        total = total + stats[group]
    count = jnp.maximum(total[0:lanes], 1.0)
    mean = total[lanes : 2 * lanes] / count
    var = total[2 * lanes : 3 * lanes] / count - mean * mean
    rate = lax.rsqrt(var + 1e-05)
    mean_line = jnp.concatenate([mean[i : i + 1] for i in range(lanes)], axis=1)
    rate_line = jnp.concatenate([rate[i : i + 1] for i in range(lanes)], axis=1)

    swap = remote(
        blocks.at[0], blocks.at[0], core_send.at[0], core_recv.at[0], other
    )

    def ahead_copy(chunk):
        return remote(
            blocks.at[0, :, pl.ds(chunk * 128, 128)],
            ahead.at[chunk],
            x_send.at[0, chunk],
            x_recv.at[0, chunk],
            before_b,
        )

    def behind_copy(chunk):
        return remote(
            ordered.at[:, pl.ds(chunk * 128, 128)],
            behind.at[chunk],
            x_send.at[1, chunk],
            x_recv.at[1, chunk],
            after_b,
        )

    def standardize(strip):
        cols = slice(strip * 128, strip * 128 + 128)
        mean_row = mean_line[:, cols]
        rate_row = rate_line[:, cols]

        def some_rows(step, carry):
            span = pl.ds(pl.multiple_of(step * 128, 128), 128)
            v = dose_v[span, cols].astype(F32)
            m = seen_v[span, cols].astype(F32)
            blocks[core, span, cols] = (m * (v - mean_row) * rate_row).astype(BF16)
            return carry

        lax.fori_loop(0, rows // 128, some_rows, 0)

    def first_core_sends():
        line_ours[0:1] = mean_line[:, 0:128]
        line_ours[1:2] = rate_line[:, 0:128]
        raw_copy(0, 2).start()
        for chunk in range(1, 4):
            standardize(chunk)
            ahead_copy(chunk).start()
        standardize(0)
        swap.start()

    def second_core_sends():
        parts = []
        for line in (mean_line, rate_line):
            for _ in range(3):
                top = line.astype(BF16)
                line = line - top.astype(F32)
                parts.append(top)
        parts = jnp.concatenate(parts + [jnp.zeros((10, width), BF16)], axis=0)
        picked = jnp.dot(parts, picks[:, 0:128], preferred_element_type=F32)
        line_ours[0:1] = picked[0:1] + picked[1:2] + picked[2:3]
        line_ours[1:2] = picked[3:4] + picked[4:5] + picked[5:6]
        raw_copy(1, 2).start()
        for strip in range(4):
            standardize(strip)
        for chunks in ((1,), (2, 3)):
            cols = slice(chunks[0] * 128, chunks[-1] * 128 + 128)
            ordered[:, cols] = jnp.dot(
                blocks[1], picks[:, cols], preferred_element_type=F32
            ).astype(BF16)
            for chunk in chunks:
                behind_copy(chunk).start()

    with jax.named_scope("standardize"):
        pl.when(core == 0)(first_core_sends)
        pl.when(core == 1)(second_core_sends)

    early = [
        Chain(
            groups,
            STRIDES[number],
            part_e.at[number],
            stage_e.at[number],
            slots_e.at[number],
            e_send.at[number],
            e_recv.at[number],
            along,
        )
        for number in range(2)
    ]
    late = [
        Chain(
            groups,
            STRIDES[2 + chunk],
            part_l.at[chunk],
            stage_l.at[chunk],
            slots_l.at[chunk],
            l_send.at[chunk],
            l_recv.at[chunk],
            along,
        )
        for chunk in range(4)
    ]

    def early_gram(number):
        if number == 1:
            with jax.named_scope("swap_wait"):
                swap.wait_recv()
        left = core if number == 0 else 0
        for strip in range(4):
            cols = slice(strip * 128, strip * 128 + 128)
            product = gram(blocks[left, :, cols], blocks[core])
            part_e[number, strip * 4 : strip * 4 + 4] = product.reshape(4, 32, 512)

    def arrived(ref, sem):
        pltpu.make_async_copy(ref, ref, sem).wait()

    def raw_standardize(side):
        raw = (raw_ahead, raw_behind)[side]
        line = (line_ahead, line_behind)[side]
        target = (ahead, behind)[side]
        with jax.named_scope("raw_wait"):
            for half in range(2):
                arrived(raw.at[half], r_recv.at[side, half])
            arrived(line, r_recv.at[side, 2])
        mean_row = line[0:1]
        rate_row = line[1:2]

        def some_rows(step, carry):
            span = pl.ds(pl.multiple_of(step * 128, 128), 128)
            v = raw[0, span].astype(F32)
            m = raw[1, span].astype(F32)
            target[0, span] = (m * (v - mean_row) * rate_row).astype(BF16)
            return carry

        lax.fori_loop(0, rows // 128, some_rows, 0)

    def late_gram(chunk):
        if chunk == 0:
            raw_standardize(0)
            raw_standardize(1)
        else:
            with jax.named_scope("ahead_wait"):
                arrived(ahead.at[chunk], x_recv.at[0, chunk])
            with jax.named_scope("behind_wait"):
                arrived(behind.at[chunk], x_recv.at[1, chunk])
        with jax.named_scope("late_gram"):
            part = part_l.at[chunk]
            for block in range(2):
                product = gram(blocks[block], ahead[chunk])
                cols = slice(block * 128, block * 128 + 128)
                part[:, :, cols] = product.reshape(16, 32, 128)
            product = gram(behind[chunk], blocks[1])
            for piece in range(4):
                cols = slice(piece * 128, piece * 128 + 128)
                part[:, piece * 8 : piece * 8 + 8, 256:384] = product[:, cols].reshape(
                    16, 8, 128
                )

    scale = 1.0 / samples
    last = chip == chips - 1

    def early_copy():
        return remote(give_e, take_e, f_send.at[0], f_recv.at[0], other)

    def late_copy(chunk):
        return remote(
            give_l.at[chunk],
            take_l.at[chunk],
            f_send.at[1 + chunk],
            f_recv.at[1 + chunk],
            other,
        )

    def back_copy(chunk):
        return remote(
            give_p.at[chunk],
            take_p.at[chunk],
            f_send.at[5 + chunk],
            f_recv.at[5 + chunk],
            before_b,
        )

    def end(number):
        if number == 0:
            out[:, 0:512] = early[0].finish() * scale
        elif number == 1:
            give_e[...] = early[1].finish() * scale
            early_copy().start()
        else:
            chunk = number - 2
            total = late[chunk].finish() * scale
            give_p[chunk] = total[:, 256:384]
            back_copy(chunk).start()
            give_l[chunk] = jnp.where(last, 0.0, total[:, 0:128])
            late_copy(chunk).start()
            cols = slice(512 + 128 * chunk, 640 + 128 * chunk)
            out[:, cols] = jnp.where(last, 0.0, total[:, 128:256])

    def first_core_end():
        arrived(take_e, f_recv.at[0])
        out[:, 512:1024] = take_e[...]
        for chunk in range(4):
            arrived(take_l.at[chunk], f_recv.at[1 + chunk])
            out[:, 1024 + 128 * chunk : 1152 + 128 * chunk] = take_l[chunk]

    def second_core_end():
        for chunk in range(4):
            arrived(take_p.at[chunk], f_recv.at[5 + chunk])
            value = jnp.where(last, 0.0, take_p[chunk])
            for piece in range(4):
                out[
                    8 * chunk : 8 * chunk + 8,
                    1024 + 128 * piece : 1152 + 128 * piece,
                ] = value[piece * 8 : piece * 8 + 8]

    def run(side):
        units = early + late
        names = ("own", "cross", "late0", "late1", "late2", "late3")
        for number, index in ORDER[side]:
            steps = units[number].levels()
            if index == 0:
                with jax.named_scope(names[number] + "_gram"):
                    if number < 2:
                        early_gram(number)
                    else:
                        late_gram(number - 2)
            with jax.named_scope(names[number] + "_" + str(index)):
                if index < len(steps):
                    for way, offset in steps[index]:
                        units[number].visit(way, offset)
                else:
                    end(number)

    def first_core():
        run(0)
        with jax.named_scope("ends"):
            first_core_end()
        swap.wait_send()
        early[0].drain()
        for chunk in range(1, 4):
            ahead_copy(chunk).wait_send()
        for number in range(3):
            raw_copy(0, number).wait_send()

    def second_core():
        run(1)
        with jax.named_scope("ends"):
            second_core_end()
        for unit in early + late:
            unit.drain()
        early_copy().wait_send()
        for chunk in range(1, 4):
            behind_copy(chunk).wait_send()
        for number in range(3):
            raw_copy(1, number).wait_send()
        for chunk in range(4):
            late_copy(chunk).wait_send()
            back_copy(chunk).wait_send()

    pl.when(core == 0)(first_core)
    pl.when(core == 1)(second_core)

    for post in posts:
        post.wait_send()


def solution(mesh):
    groups, snps = mesh.shape["samp"], mesh.shape["snp"]

    def local(dosages, observed):
        rows, width = dosages.shape
        vmem = pltpu.VMEM
        dma = pltpu.SemaphoreType.DMA
        return pl.pallas_call(
            functools.partial(band_kernel, groups, snps // 2),
            out_shape=jax.ShapeDtypeStruct((width // groups, 3 * width), F32),
            in_specs=[pl.BlockSpec(memory_space=pl.ANY)] * 2,
            out_specs=pl.BlockSpec(memory_space=pltpu.VMEM),
            scratch_shapes=[
                vmem((rows, width), BF16),
                vmem((rows, width), jnp.int32),
                vmem((groups, 16, 128), F32),
                vmem((2, rows, width), BF16),
                vmem((width, width), BF16),
                vmem((rows, width), BF16),
                vmem((4, rows, 128), BF16),
                vmem((4, rows, 128), BF16),
                vmem((2, rows, 128), BF16),
                vmem((2, rows, 128), BF16),
                vmem((2, rows, 128), BF16),
                vmem((8, 128), F32),
                vmem((8, 128), F32),
                vmem((8, 128), F32),
                vmem((2, groups, 32, 512), F32),
                vmem((4, groups, 32, 384), F32),
                vmem((2, 2, 8, 32, 512), jnp.int16),
                vmem((4, 2, 8, 32, 384), jnp.int16),
                vmem((2, 2, 8, 32, 512), jnp.int16),
                vmem((4, 2, 8, 32, 384), jnp.int16),
                vmem((32, 512), F32),
                vmem((4, 32, 128), F32),
                vmem((4, 32, 128), F32),
                vmem((32, 512), F32),
                vmem((4, 32, 128), F32),
                vmem((4, 32, 128), F32),
                dma((2, 6)),
                dma((groups,)),
                dma((groups,)),
                dma((1,)),
                dma((1,)),
                dma((2, 4)),
                dma((2, 4)),
                dma((2, 3)),
                dma((2, 3)),
                dma((2, 2, 8)),
                dma((2, 2, 8)),
                dma((4, 2, 8)),
                dma((4, 2, 8)),
                dma((9,)),
                dma((9,)),
            ],
            compiler_params=pltpu.CompilerParams(
                collective_id=0,
                has_side_effects=True,
                vmem_limit_bytes=56 * 2**20,
            ),
            cost_estimate=pl.CostEstimate(
                flops=2 * 3 * rows * width * width,
                bytes_accessed=6 * rows * width,
                transcendentals=0,
            ),
            name="band",
        )(dosages, observed)

    return jax.shard_map(
        local,
        mesh=mesh,
        in_specs=(P("samp", "snp"), P("samp", "snp")),
        out_specs=P(("snp", "samp"), None),
        check_vma=False,
    )
```

```python
import functools
import math

import jax
import jax.numpy as jnp
from jax import lax
from jax.experimental import pallas as pl
from jax.experimental.pallas import tpu as pltpu
from jax.sharding import PartitionSpec as P

MESH = pl.DeviceIdType.MESH
F32 = jnp.float32
BF16 = jnp.bfloat16

STEPS = 1650.0
FINE = 4096.0


OWN_STRIDE = 1
CROSS = 1
CROSS_STRIDE = 1
LATE = ((0, 0, 32, 1), (1, 0, 32, 1), (2, 0, 32, 1), (3, 0, 32, 2))
ORDER = (
    ((0, 0), (0, 1), (0, 2), (0, 3), (0, 4), (0, 5), (0, 6), (0, 7), (0, 8),),
    ((0, 0), (0, 1), (1, 0), (3, 0), (2, 0), (1, 1), (3, 1), (0, 2), (4, 0), (2, 1), (1, 2), (3, 2), (0, 3), (4, 1), (2, 2), (1, 3), (5, 0), (4, 2), (3, 3), (2, 3), (1, 4), (0, 4), (4, 3), (3, 4), (2, 4), (1, 5), (0, 5), (5, 1), (4, 4), (3, 5), (2, 5), (1, 6), (0, 6), (4, 5), (5, 2), (3, 6), (2, 6), (1, 7), (0, 7), (4, 6), (3, 7), (2, 7), (5, 3), (1, 8), (0, 8), (4, 7), (3, 8), (2, 8), (5, 4), (4, 8),),
)


def encode(x):
    q = jnp.minimum(STEPS * jnp.log(1.0 + FINE * jnp.abs(x)) + 0.5, 32767.0).astype(
        jnp.int32
    )
    return jnp.where(x < 0.0, -q, q).astype(jnp.int16)


def decode(q):
    f = q.astype(jnp.int32).astype(F32)
    a = (jnp.exp(jnp.abs(f) * (1.0 / STEPS)) - 1.0) * (1.0 / FINE)
    return jnp.where(f < 0.0, -a, a)


def gram(left, right):
    return lax.dot_general(
        left, right, (((0,), (0,)), ((), ())), preferred_element_type=F32
    )


class Chain:
    def __init__(self, groups, stride, part, stage, slots, send, recv, device, last=None):
        self.groups = groups
        self.reach = (groups // 2, groups - 1 - groups // 2)
        self.stride = tuple(min(stride, reach) for reach in self.reach)
        self.part, self.stage, self.slots = part, stage, slots
        self.send, self.recv, self.device, self.last = send, recv, device, last

    def slot(self, way, number):
        return way * self.reach[0] + number - 1

    def hops(self, way, offset, source):
        stride, reach = self.stride[way], self.reach[way]
        sign = 1 if way == 0 else -1
        slot = offset - stride if offset > stride else reach - stride + offset
        slot = self.slot(way, slot)
        if offset > stride or self.last is None:
            return [
                pltpu.make_async_remote_copy(
                    src_ref=source,
                    dst_ref=self.slots.at[slot],
                    send_sem=self.send,
                    recv_sem=self.recv.at[slot],
                    device_id=self.device(sign * min(stride, offset)),
                    device_id_type=MESH,
                )
            ]
        return self.last(slot, sign * offset, source)

    def arrival(self, way, number):
        slot = self.slot(way, number)
        ref = self.slots.at[slot]
        return pltpu.make_async_copy(ref, ref, self.recv.at[slot])

    def own(self, way, offset):
        me = lax.axis_index("samp")
        sign = 1 if way == 0 else -1
        return lax.rem(me + sign * offset + self.groups, self.groups)

    def source(self, way, offset):
        reach, stride = self.reach[way], self.stride[way]
        if offset + stride > reach:
            return self.stage.at[way, reach - offset]
        return self.slots.at[self.slot(way, offset)]

    def last_slots(self):
        return [
            self.slot(way, self.reach[way] - self.stride[way] + near)
            for near in range(1, max(self.stride) + 1)
            for way in (0, 1)
            if near <= self.stride[way]
        ]

    def visit(self, way, offset):
        reach, stride = self.reach[way], self.stride[way]
        ref = self.source(way, offset)
        total = self.part[self.own(way, offset)]
        if offset + stride <= reach:
            self.arrival(way, offset).wait()
            total = total + decode(ref[...])
        ref[...] = encode(total)
        for copy in self.hops(way, offset, ref):
            copy.start()

    def levels(self):
        steps = []
        for way in (0, 1):
            for place, offset in enumerate(range(self.reach[way], 0, -1)):
                number = place // self.stride[way]
                if number == len(steps):
                    steps.append([])
                steps[number].append((place, way, offset))
        return [[visit[1:] for visit in sorted(step)] for step in steps]

    def finish(self):
        total = self.part[lax.axis_index("samp")]
        for slot in self.last_slots():
            ref = self.slots.at[slot]
            pltpu.make_async_copy(ref, ref, self.recv.at[slot]).wait()
            total = total + decode(ref[...])
        return total

    def drain(self, last_send=None):
        whole, end = sum(self.reach), sum(self.stride)
        if last_send is not None:
            ref = self.slots.at[pl.ds(0, end)]
            pltpu.make_async_copy(ref, ref, last_send).wait()
            whole -= end
        if whole:
            ref = self.slots.at[pl.ds(0, whole)]
            pltpu.make_async_copy(ref, ref, self.send).wait()


LATE_ENDS = [
    Chain(16, unit[3], None, None, None, None, None, None).last_slots() for unit in LATE
]
LATE_FROM = [sum(len(e) for e in LATE_ENDS[:n]) for n in range(len(LATE) + 1)]


def band_kernel(
    groups,
    chips,
    dosages,
    observed,
    out,
    dose_v,
    seen_v,
    stats,
    blocks,
    picks,
    ordered,
    ahead,
    behind,
    raw_ours,
    raw_ahead,
    raw_behind,
    line_ours,
    line_ahead,
    line_behind,
    part_e,
    part_l,
    stage_e,
    stage_l,
    slots_e,
    slots_l,
    ours_l,
    home_l,
    give_e,
    take_e,
    load_sem,
    stat_send,
    stat_recv,
    core_send,
    core_recv,
    x_send,
    x_recv,
    r_send,
    r_recv,
    e_send,
    e_recv,
    l_send,
    l_recv,
    t_send,
    t_recv,
    h_send,
    h_recv,
    f_send,
    f_recv,
):
    snp, me = lax.axis_index("snp"), lax.axis_index("samp")
    core = lax.rem(snp, 2)
    chip = lax.div(snp, 2)
    rows, width = dose_v.shape
    samples = rows * groups
    count_snp = 2 * chips

    def along(distance):
        return (snp, lax.rem(me + distance + groups, groups))

    other = (snp + 1 - 2 * core, me)
    before_b = (lax.rem(2 * chip + count_snp - 1, count_snp), me)
    after_b = (lax.rem(2 * chip + 3, count_snp), me)
    after_a = (lax.rem(2 * chip + 2, count_snp), me)

    def remote(src, dst, send, recv, device):
        return pltpu.make_async_remote_copy(
            src_ref=src,
            dst_ref=dst,
            send_sem=send,
            recv_sem=recv,
            device_id=device,
            device_id_type=MESH,
        )

    half = groups // 2
    order = [half] + [sign * d for d in range(half - 1, 0, -1) for sign in (1, -1)]
    barrier = pltpu.get_barrier_semaphore()

    def greet(peers):
        for peer in peers:
            pl.semaphore_signal(barrier, inc=1, device_id=peer, device_id_type=MESH)

    def beside(device, distance):
        return (device[0], lax.rem(me + distance + groups, groups))

    greet([along(d) for d in order] + [other, before_b])
    pl.when(core == 1)(lambda: greet([after_a, after_b]))

    pieces = load_sem.shape[1]
    high = rows // pieces

    def load(piece):
        span = pl.ds(piece * high, high)
        return (
            pltpu.make_async_copy(
                dosages.at[span], dose_v.at[span], load_sem.at[0, piece]
            ),
            pltpu.make_async_copy(
                observed.at[span], seen_v.at[span], load_sem.at[1, piece]
            ),
        )


    for piece in range(pieces):
        for copy in load(piece):
            copy.start()

    def make_picks():
        line = lax.broadcasted_iota(jnp.int32, (width, width), 0)
        col = lax.broadcasted_iota(jnp.int32, (width, width), 1)
        from_row = 32 * ((col >> 3) & 15) + 8 * (col >> 7) + (col & 7)
        picks[...] = jnp.where(line == from_row, 1.0, 0.0).astype(BF16)

    def add_rows(step, carry):
        span = pl.ds(pl.multiple_of(step * 32, 32), 32)
        v = dose_v[span].astype(F32)
        m = seen_v[span].astype(F32)
        mv = m * v
        sums = []
        for acc, term in zip(carry, (m, mv, mv * v)):
            sums.append(acc + jnp.sum(term.reshape(4, 8, width), axis=0))
        return tuple(sums)

    carry = tuple(jnp.zeros((8, width), F32) for _ in range(3))
    for piece in range(pieces):
        for copy in load(piece):
            copy.wait()
        carry = lax.fori_loop(
            piece * high // 32, (piece + 1) * high // 32, add_rows, carry
        )
    lanes = width // 128
    for kind, acc in enumerate(carry):
        line = jnp.sum(acc, axis=0, keepdims=True)
        for lane in range(lanes):
            row = kind * lanes + lane
            stats[me, row : row + 1, :] = line[:, lane * 128 : lane * 128 + 128]

    def raw_first():
        raw_ours[0] = dose_v[:, 0:128]
        raw_ours[1] = seen_v[:, 0:128].astype(F32).astype(BF16)

    def raw_second():
        make_picks()
        pick = picks[:, 0:128]
        raw_ours[0] = jnp.dot(
            dose_v[...], pick, preferred_element_type=F32
        ).astype(BF16)
        raw_ours[1] = jnp.dot(
            seen_v[...].astype(F32).astype(BF16), pick, preferred_element_type=F32
        ).astype(BF16)

    def raw_copy(side, number):
        return remote(
            (raw_ours, line_ours)[number],
            ((raw_ahead, raw_behind), (line_ahead, line_behind))[number][side],
            r_send.at[number],
            r_recv.at[side, number],
            (before_b, after_b)[side],
        )

    with jax.named_scope("raw"):
        pl.when(core == 0)(raw_first)
        pl.when(core == 1)(raw_second)
    with jax.named_scope("entry_wait"):
        pl.semaphore_wait(barrier, groups + 1 + 2 * core)

    posts = []
    for distance in order:
        posts.append(
            remote(
                stats.at[me],
                stats.at[me],
                stat_send,
                stat_recv.at[lax.rem(distance + groups, groups)],
                along(distance),
            )
        )
        posts[-1].start()

    pl.when(core == 0)(lambda: raw_copy(0, 0).start())
    pl.when(core == 1)(lambda: raw_copy(1, 0).start())
    with jax.named_scope("stats_wait"):
        for distance in range(1, groups):
            origin = lax.rem(me - distance + groups, groups)
            ref = stats.at[origin]
            pltpu.make_async_copy(ref, ref, stat_recv.at[distance]).wait()
    total = stats[0]
    for group in range(1, groups):
        total = total + stats[group]
    count = jnp.maximum(total[0:lanes], 1.0)
    mean = total[lanes : 2 * lanes] / count
    var = total[2 * lanes : 3 * lanes] / count - mean * mean
    rate = lax.rsqrt(var + 1e-05)
    mean_line = jnp.concatenate([mean[i : i + 1] for i in range(lanes)], axis=1)
    rate_line = jnp.concatenate([rate[i : i + 1] for i in range(lanes)], axis=1)

    def arrived(ref, sem):
        pltpu.make_async_copy(ref, ref, sem).wait()

    def swap(block):
        return remote(
            blocks.at[block],
            blocks.at[block],
            core_send,
            core_recv,
            other,
        )

    def ahead_copy(chunk):
        return remote(
            blocks.at[0, :, pl.ds(chunk * 128, 128)],
            ahead.at[chunk],
            x_send,
            x_recv.at[0, chunk - 1],
            before_b,
        )

    def behind_copy(chunk):
        return remote(
            ordered.at[:, pl.ds(chunk * 128, 128)],
            behind.at[chunk],
            x_send,
            x_recv.at[1, chunk - 1],
            after_b,
        )

    def standardize(strip):
        cols = slice(strip * 128, strip * 128 + 128)
        mean_row = mean_line[:, cols]
        rate_row = rate_line[:, cols]

        def some_rows(step, carry):
            span = pl.ds(pl.multiple_of(step * 128, 128), 128)
            v = dose_v[span, cols].astype(F32)
            m = seen_v[span, cols].astype(F32)
            blocks[core, span, cols] = (m * (v - mean_row) * rate_row).astype(BF16)
            return carry

        lax.fori_loop(0, rows // 128, some_rows, 0)

    def first_core_sends():
        line_ours[0:1] = mean_line[:, 0:128]
        line_ours[1:2] = rate_line[:, 0:128]
        raw_copy(0, 1).start()
        for chunk in range(1, 4):
            standardize(chunk)
            ahead_copy(chunk).start()
        standardize(0)
        swap(0).start()

    def second_core_sends():
        parts = []
        for line in (mean_line, rate_line):
            for _ in range(3):
                top = line.astype(BF16)
                line = line - top.astype(F32)
                parts.append(top)
        parts = jnp.concatenate(parts + [jnp.zeros((10, width), BF16)], axis=0)
        picked = jnp.dot(parts, picks[:, 0:128], preferred_element_type=F32)
        line_ours[0:1] = picked[0:1] + picked[1:2] + picked[2:3]
        line_ours[1:2] = picked[3:4] + picked[4:5] + picked[5:6]
        raw_copy(1, 1).start()
        for strip in range(4):
            standardize(strip)
        for chunks in ((1,), (2, 3)):
            cols = slice(chunks[0] * 128, chunks[-1] * 128 + 128)
            ordered[:, cols] = jnp.dot(
                blocks[1], picks[:, cols], preferred_element_type=F32
            ).astype(BF16)
            for chunk in chunks:
                behind_copy(chunk).start()
            if CROSS == 0 and chunks[0] == 1:
                swap(1).start()

    with jax.named_scope("standardize"):
        pl.when(core == 0)(first_core_sends)
        pl.when(core == 1)(second_core_sends)

    early = [
        Chain(
            groups,
            (OWN_STRIDE, CROSS_STRIDE)[number],
            part_e.at[number],
            stage_e.at[number],
            slots_e.at[number],
            e_send.at[number],
            e_recv.at[number],
            along,
        )
        for number in range(2)
    ]
    def end_sem(unit, third, slot):
        if third < 2:
            return l_recv.at[unit, slot]
        return t_recv.at[LATE_ENDS[unit].index(slot) + LATE_FROM[unit]]

    def thirds(unit):
        chunk, first, high, _ = LATE[unit]
        line = pl.ds(first, high)

        def last(slot, distance, source):
            homes = (beside(other, distance), along(distance), beside(before_b, distance))
            return [
                remote(
                    source.at[:, pl.ds(128 * third, 128)],
                    slots_l.at[chunk, slot, line, pl.ds(128 * third, 128)],
                    t_send.at[unit],
                    end_sem(unit, third, slot),
                    homes[third],
                )
                for third in range(3)
            ]

        return last

    late = [
        Chain(
            groups,
            stride,
            part_l.at[chunk, :, pl.ds(first, high)],
            stage_l.at[chunk, :, :, pl.ds(first, high)],
            slots_l.at[chunk, :, pl.ds(first, high)],
            l_send.at[unit],
            l_recv.at[unit],
            along,
            thirds(unit),
        )
        for unit, (chunk, first, high, stride) in enumerate(LATE)
    ]

    def own_term(chunk, third):
        cols = pl.ds(128 * third, 128)
        return remote(
            ours_l.at[chunk, :, cols],
            home_l.at[chunk, :, cols],
            h_send,
            h_recv.at[chunk],
            other if third == 0 else before_b,
        )

    def landed(unit, third):
        chunk, first, high, _ = LATE[unit]
        total = jnp.zeros((high, 128), F32)
        for slot in late[unit].last_slots():
            ref = slots_l.at[
                chunk, slot, pl.ds(first, high), pl.ds(128 * third, 128)
            ]
            arrived(ref, end_sem(unit, third, slot))
            total = total + decode(ref[...])
        return total

    def early_gram(number):
        left, right = (core, core) if number == 0 else (0, 1)
        for strip in range(4):
            cols = slice(strip * 128, strip * 128 + 128)
            product = gram(blocks[left, :, cols], blocks[right])
            part_e[number, strip * 4 : strip * 4 + 4] = product.reshape(4, 32, 512)

    def raw_standardize(side):
        raw = (raw_ahead, raw_behind)[side]
        line = (line_ahead, line_behind)[side]
        target = (ahead, behind)[side]
        with jax.named_scope("raw_wait"):
            arrived(raw, r_recv.at[side, 0])
            arrived(line, r_recv.at[side, 1])
        mean_row = line[0:1]
        rate_row = line[1:2]

        def some_rows(step, carry):
            span = pl.ds(pl.multiple_of(step * 128, 128), 128)
            v = raw[0, span].astype(F32)
            m = raw[1, span].astype(F32)
            target[0, span] = (m * (v - mean_row) * rate_row).astype(BF16)
            return carry

        lax.fori_loop(0, rows // 128, some_rows, 0)

    def late_gram(chunk):
        if chunk == 0:
            raw_standardize(0)
            raw_standardize(1)
        else:
            with jax.named_scope("ahead_wait"):
                arrived(ahead.at[chunk], x_recv.at[0, chunk - 1])
            with jax.named_scope("behind_wait"):
                arrived(behind.at[chunk], x_recv.at[1, chunk - 1])
        with jax.named_scope("late_gram"):
            part = part_l.at[chunk]
            for block in range(2):
                product = gram(blocks[block], ahead[chunk])
                cols = slice(block * 128, block * 128 + 128)
                part[:, :, cols] = product.reshape(16, 32, 128)
            product = gram(behind[chunk], blocks[1])
            for piece in range(4):
                cols = slice(piece * 128, piece * 128 + 128)
                part[:, piece * 8 : piece * 8 + 8, 256:384] = product[:, cols].reshape(
                    16, 8, 128
                )
            ours_l[chunk] = encode(part[me])
            own_term(chunk, 0).start()
            own_term(chunk, 2).start()

    scale = 1.0 / samples
    last = chip == chips - 1

    def early_copy():
        return remote(give_e, take_e, f_send.at[0], f_recv.at[0], other)

    def end(number):
        if number == 0:
            out[:, 0:512] = early[0].finish() * scale
        elif number == 1:
            total = early[1].finish() * scale
            if CROSS == 0:
                out[:, 512:1024] = total
            else:
                give_e[...] = total
                early_copy().start()
        else:
            unit = number - 2
            chunk, first, high, _ = LATE[unit]
            line = slice(first, first + high)
            total = landed(unit, 1) + part_l[chunk, me, line, 128:256]
            cols = slice(512 + 128 * chunk, 640 + 128 * chunk)
            out[line, cols] = jnp.where(last, 0.0, total * scale)

    def end_first(unit):
        chunk, first, high, _ = LATE[unit]
        line = slice(first, first + high)
        if unit == 0 or LATE[unit - 1][0] != chunk:
            arrived(home_l.at[chunk, :, pl.ds(0, 128)], h_recv.at[chunk])
        total = landed(unit, 0) + decode(home_l[chunk, line, 0:128])
        cols = slice(1024 + 128 * chunk, 1152 + 128 * chunk)
        out[line, cols] = jnp.where(last, 0.0, total * scale)

    def end_second(unit):
        chunk, first, high, _ = LATE[unit]
        line = slice(first, first + high)
        if unit == 0 or LATE[unit - 1][0] != chunk:
            arrived(home_l.at[chunk, :, pl.ds(256, 128)], h_recv.at[chunk])
        total = landed(unit, 2) + decode(home_l[chunk, line, 256:384])
        value = jnp.where(last, 0.0, total * scale)
        for piece in range(high // 8):
            cols = 1024 + 128 * (first // 8 + piece)
            out[8 * chunk : 8 * chunk + 8, cols : cols + 128] = value[
                piece * 8 : piece * 8 + 8
            ]

    def run(side):
        units = early + late
        swapped = False
        for number, index in ORDER[side]:
            name = ("own", "cross")[number] if number < 2 else f"late{number - 2}"
            steps = units[number].levels()
            if number > 0 and not swapped:
                swapped = True
                if side == 1 or CROSS == 0:
                    with jax.named_scope("swap_wait"):
                        swap(1 - side).wait_recv()
            if index == 0:
                with jax.named_scope(name + "_gram"):
                    if number < 2:
                        early_gram(number)
                    elif number == 2 or LATE[number - 3][0] != LATE[number - 2][0]:
                        late_gram(LATE[number - 2][0])
            with jax.named_scope(f"{name}_{index}"):
                if index < len(steps):
                    for way, offset in steps[index]:
                        units[number].visit(way, offset)
                else:
                    end(number)

    def first_core():
        run(0)
        with jax.named_scope("ends"):
            for unit in range(len(LATE)):
                end_first(unit)
            if CROSS == 1:
                arrived(take_e, f_recv.at[0])
                out[:, 512:1024] = take_e[...]
        swap(0).wait_send()
        for chain in early[: 2 - CROSS]:
            chain.drain()
        arrived(ahead.at[pl.ds(0, 3)], x_send)
        for number in range(2):
            raw_copy(0, number).wait_send()

    def second_core():
        run(1)
        with jax.named_scope("ends"):
            for unit in range(len(LATE)):
                end_second(unit)
        for chain in early[: 1 + CROSS]:
            chain.drain()
        for unit, chain in enumerate(late):
            chain.drain(t_send.at[unit])
        if CROSS == 1:
            early_copy().wait_send()
        else:
            swap(1).wait_send()
        arrived(ahead.at[pl.ds(0, 3)], x_send)
        for number in range(2):
            raw_copy(1, number).wait_send()
        arrived(ours_l.at[:, :, pl.ds(0, 256)], h_send)

    pl.when(core == 0)(first_core)
    pl.when(core == 1)(second_core)

    sent = stats.at[pl.ds(0, groups - 1)]
    pltpu.make_async_copy(sent, sent, stat_send).wait()


def solution(mesh):
    groups, snps = mesh.shape["samp"], mesh.shape["snp"]

    def local(dosages, observed):
        rows, width = dosages.shape
        vmem = pltpu.VMEM
        dma = pltpu.SemaphoreType.DMA
        return pl.pallas_call(
            functools.partial(band_kernel, groups, snps // 2),
            out_shape=jax.ShapeDtypeStruct((width // groups, 3 * width), F32),
            in_specs=[pl.BlockSpec(memory_space=pl.ANY)] * 2,
            out_specs=pl.BlockSpec(memory_space=pltpu.VMEM),
            scratch_shapes=[
                vmem((rows, width), BF16),
                vmem((rows, width), jnp.int32),
                vmem((groups, 12, 128), F32),
                vmem((2, rows, width), BF16),
                vmem((width, width), BF16),
                vmem((rows, width), BF16),
                vmem((4, rows, 128), BF16),
                vmem((4, rows, 128), BF16),
                vmem((2, rows, 128), BF16),
                vmem((2, rows, 128), BF16),
                vmem((2, rows, 128), BF16),
                vmem((8, 128), F32),
                vmem((8, 128), F32),
                vmem((8, 128), F32),
                vmem((2, groups, 32, 512), F32),
                vmem((4, groups, 32, 384), F32),
                vmem((2, 2, 8, 32, 512), jnp.int16),
                vmem((4, 2, 8, 32, 384), jnp.int16),
                vmem((2, 15, 32, 512), jnp.int16),
                vmem((4, 15, 32, 384), jnp.int16),
                vmem((4, 32, 384), jnp.int16),
                vmem((4, 32, 384), jnp.int16),
                vmem((32, 512), F32),
                vmem((32, 512), F32),
                dma((2, 4)),
                dma,
                dma((groups,)),
                dma,
                dma,
                dma,
                dma((2, 3)),
                dma((2,)),
                dma((2, 2)),
                dma((2,)),
                dma((2, 15)),
                dma((len(LATE),)),
                dma((len(LATE), 15)),
                dma((len(LATE),)),
                dma((LATE_FROM[-1],)),
                dma,
                dma((4,)),
                dma((1,)),
                dma((1,)),
            ],
            compiler_params=pltpu.CompilerParams(
                collective_id=0,
                has_side_effects=True,
                vmem_limit_bytes=56 * 2**20,
            ),
            cost_estimate=pl.CostEstimate(
                flops=2 * 3 * rows * width * width,
                bytes_accessed=6 * rows * width,
                transcendentals=0,
            ),
            name="band",
        )(dosages, observed)

    return jax.shard_map(
        local,
        mesh=mesh,
        in_specs=(P("samp", "snp"), P("samp", "snp")),
        out_specs=P(("snp", "samp"), None),
        check_vma=False,
    )
```

```python
import functools
import math

import jax
import jax.numpy as jnp
from jax import lax
from jax.experimental import pallas as pl
from jax.experimental.pallas import tpu as pltpu
from jax.sharding import PartitionSpec as P

MESH = pl.DeviceIdType.MESH
F32 = jnp.float32
BF16 = jnp.bfloat16

STEPS = 1650.0
FINE = 4096.0


OWN_STRIDE = 2
CROSS = 1
CROSS_STRIDE = 1
LATE = ((0, 0, 32, 1), (1, 0, 32, 1), (2, 0, 32, 2), (3, 0, 32, 2))
ORDER = (
    ((0, 0), (0, 1), (0, 2), (0, 3), (0, 4),),
    ((0, 0), (1, 0), (2, 0), (3, 0), (1, 1), (0, 1), (2, 1), (4, 0), (3, 1), (1, 2), (2, 2), (0, 2), (5, 0), (3, 2), (2, 3), (1, 3), (4, 1), (0, 3), (3, 3), (2, 4), (1, 4), (5, 1), (3, 4), (2, 5), (4, 2), (0, 4), (1, 5), (5, 2), (3, 5), (2, 6), (1, 6), (4, 3), (3, 6), (2, 7), (5, 3), (1, 7), (4, 4), (3, 7), (2, 8), (1, 8), (5, 4), (3, 8),),
)


def encode(x):
    q = jnp.minimum(STEPS * jnp.log(1.0 + FINE * jnp.abs(x)) + 0.5, 32767.0).astype(
        jnp.int32
    )
    return jnp.where(x < 0.0, -q, q).astype(jnp.int16)


def decode(q):
    f = q.astype(jnp.int32).astype(F32)
    a = (jnp.exp(jnp.abs(f) * (1.0 / STEPS)) - 1.0) * (1.0 / FINE)
    return jnp.where(f < 0.0, -a, a)


def gram(left, right):
    return lax.dot_general(
        left, right, (((0,), (0,)), ((), ())), preferred_element_type=F32
    )


class Chain:
    def __init__(self, groups, stride, part, stage, slots, send, recv, device, last=None):
        self.groups = groups
        self.reach = (groups // 2, groups - 1 - groups // 2)
        self.stride = tuple(min(stride, reach) for reach in self.reach)
        self.part, self.stage, self.slots = part, stage, slots
        self.send, self.recv, self.device, self.last = send, recv, device, last

    def slot(self, way, number):
        return way * self.reach[0] + number - 1

    def hops(self, way, offset, source):
        stride, reach = self.stride[way], self.reach[way]
        sign = 1 if way == 0 else -1
        slot = offset - stride if offset > stride else reach - stride + offset
        slot = self.slot(way, slot)
        if offset > stride or self.last is None:
            return [
                pltpu.make_async_remote_copy(
                    src_ref=source,
                    dst_ref=self.slots.at[slot],
                    send_sem=self.send,
                    recv_sem=self.recv.at[slot],
                    device_id=self.device(sign * min(stride, offset)),
                    device_id_type=MESH,
                )
            ]
        return self.last(slot, sign * offset, source)

    def arrival(self, way, number):
        slot = self.slot(way, number)
        ref = self.slots.at[slot]
        return pltpu.make_async_copy(ref, ref, self.recv.at[slot])

    def own(self, way, offset):
        me = lax.axis_index("samp")
        sign = 1 if way == 0 else -1
        return lax.rem(me + sign * offset + self.groups, self.groups)

    def source(self, way, offset):
        reach, stride = self.reach[way], self.stride[way]
        if offset + stride > reach:
            return self.stage.at[way, reach - offset]
        return self.slots.at[self.slot(way, offset)]

    def last_slots(self):
        return [
            self.slot(way, self.reach[way] - self.stride[way] + near)
            for near in range(1, max(self.stride) + 1)
            for way in (0, 1)
            if near <= self.stride[way]
        ]

    def visit(self, way, offset):
        reach, stride = self.reach[way], self.stride[way]
        ref = self.source(way, offset)
        total = self.part[self.own(way, offset)]
        if offset + stride <= reach:
            self.arrival(way, offset).wait()
            total = total + decode(ref[...])
        ref[...] = encode(total)
        for copy in self.hops(way, offset, ref):
            copy.start()

    def levels(self):
        steps = []
        for way in (0, 1):
            for place, offset in enumerate(range(self.reach[way], 0, -1)):
                number = place // self.stride[way]
                if number == len(steps):
                    steps.append([])
                steps[number].append((place, way, offset))
        return [[visit[1:] for visit in sorted(step)] for step in steps]

    def finish(self):
        total = self.part[lax.axis_index("samp")]
        for slot in self.last_slots():
            ref = self.slots.at[slot]
            pltpu.make_async_copy(ref, ref, self.recv.at[slot]).wait()
            total = total + decode(ref[...])
        return total

    def drain(self, last_send=None):
        whole, end = sum(self.reach), sum(self.stride)
        if last_send is not None:
            ref = self.slots.at[pl.ds(0, end)]
            pltpu.make_async_copy(ref, ref, last_send).wait()
            whole -= end
        if whole:
            ref = self.slots.at[pl.ds(0, whole)]
            pltpu.make_async_copy(ref, ref, self.send).wait()


LATE_ENDS = [
    Chain(16, unit[3], None, None, None, None, None, None).last_slots() for unit in LATE
]
LATE_FROM = [sum(len(e) for e in LATE_ENDS[:n]) for n in range(len(LATE) + 1)]


def band_kernel(
    groups,
    chips,
    dosages,
    observed,
    out,
    dose_v,
    seen_v,
    stats,
    blocks,
    picks,
    ordered,
    ahead,
    behind,
    raw_ours,
    raw_rest,
    raw_ahead,
    raw_behind,
    line_ours,
    line_ahead,
    line_behind,
    part_e,
    part_l,
    stage_e,
    stage_l,
    slots_e,
    slots_l,
    ours_l,
    home_l,
    give_e,
    take_e,
    load_sem,
    stat_send,
    stat_recv,
    core_send,
    core_recv,
    x_send,
    x_recv,
    r_send,
    r_recv,
    e_send,
    e_recv,
    l_send,
    l_recv,
    t_send,
    t_recv,
    h_send,
    h_recv,
    f_send,
    f_recv,
):
    snp, me = lax.axis_index("snp"), lax.axis_index("samp")
    core = lax.rem(snp, 2)
    chip = lax.div(snp, 2)
    rows, width = dose_v.shape
    samples = rows * groups
    count_snp = 2 * chips

    def along(distance):
        return (snp, lax.rem(me + distance + groups, groups))

    other = (snp + 1 - 2 * core, me)
    before_b = (lax.rem(2 * chip + count_snp - 1, count_snp), me)
    after_b = (lax.rem(2 * chip + 3, count_snp), me)
    after_a = (lax.rem(2 * chip + 2, count_snp), me)

    has_before, has_after = chip > 0, chip < chips - 1
    sends_ahead = jnp.logical_and(core == 0, has_before)
    sends_behind = jnp.logical_and(core == 1, has_after)

    def remote(src, dst, send, recv, device):
        return pltpu.make_async_remote_copy(
            src_ref=src,
            dst_ref=dst,
            send_sem=send,
            recv_sem=recv,
            device_id=device,
            device_id_type=MESH,
        )

    half = groups // 2
    order = [half] + [sign * d for d in range(half - 1, 0, -1) for sign in (1, -1)]
    barrier = pltpu.get_barrier_semaphore()

    def greet(peers):
        for peer in peers:
            pl.semaphore_signal(barrier, inc=1, device_id=peer, device_id_type=MESH)

    def beside(device, distance):
        return (device[0], lax.rem(me + distance + groups, groups))

    greet([along(d) for d in order] + [other, before_b])
    pl.when(core == 1)(lambda: greet([after_a, after_b]))

    pieces = load_sem.shape[1]
    high = rows // pieces

    def load(piece):
        span = pl.ds(piece * high, high)
        return (
            pltpu.make_async_copy(
                dosages.at[span], dose_v.at[span], load_sem.at[0, piece]
            ),
            pltpu.make_async_copy(
                observed.at[span], seen_v.at[span], load_sem.at[1, piece]
            ),
        )


    for piece in range(pieces):
        for copy in load(piece):
            copy.start()

    def make_picks():
        line = lax.broadcasted_iota(jnp.int32, (width, width), 0)
        col = lax.broadcasted_iota(jnp.int32, (width, width), 1)
        from_row = 32 * ((col >> 3) & 15) + 8 * (col >> 7) + (col & 7)
        picks[...] = jnp.where(line == from_row, 1.0, 0.0).astype(BF16)

    def add_rows(step, carry):
        span = pl.ds(pl.multiple_of(step * 32, 32), 32)
        v = dose_v[span].astype(F32)
        m = seen_v[span].astype(F32)
        mv = m * v
        sums = []
        for acc, term in zip(carry, (m, mv, mv * v)):
            sums.append(acc + jnp.sum(term.reshape(4, 8, width), axis=0))
        return tuple(sums)

    carry = tuple(jnp.zeros((8, width), F32) for _ in range(3))
    for piece in range(pieces):
        for copy in load(piece):
            copy.wait()
        carry = lax.fori_loop(
            piece * high // 32, (piece + 1) * high // 32, add_rows, carry
        )
    lanes = width // 128
    for kind, acc in enumerate(carry):
        line = jnp.sum(acc, axis=0, keepdims=True)
        for lane in range(lanes):
            row = kind * lanes + lane
            stats[me, row : row + 1, :] = line[:, lane * 128 : lane * 128 + 128]

    def raw_first():
        raw_ours[0] = dose_v[:, 0:128]
        raw_ours[1] = seen_v[:, 0:128].astype(F32).astype(BF16)
        pl.when(has_before)(raw_copy(0, 0).start)

    def raw_second():
        ordered[...] = seen_v[...].astype(F32).astype(BF16)
        first = picks[:, 0:128]
        raw_ours[0] = jnp.dot(
            dose_v[...], first, preferred_element_type=F32
        ).astype(BF16)
        raw_ours[1] = jnp.dot(
            ordered[...], first, preferred_element_type=F32
        ).astype(BF16)
        pl.when(has_after)(raw_copy(1, 0).start)
        for pair in (slice(128, 256), slice(256, 512)):
            cols = slice(pair.start - 128, pair.stop - 128)
            raw_rest[0, :, cols] = jnp.dot(
                dose_v[...], picks[:, pair], preferred_element_type=F32
            ).astype(BF16)
            raw_rest[1, :, cols] = jnp.dot(
                ordered[...], picks[:, pair], preferred_element_type=F32
            ).astype(BF16)

    def raw_copy(side, number):
        return remote(
            (raw_ours, line_ours)[number],
            ((raw_ahead, raw_behind), (line_ahead, line_behind))[number][side],
            r_send.at[number],
            r_recv.at[side, number],
            (before_b, after_b)[side],
        )

    def no_after():
        ahead[...] = jnp.zeros(ahead.shape, BF16)

    def no_before():
        behind[...] = jnp.zeros(behind.shape, BF16)

    pl.when(jnp.logical_and(core == 1, jnp.logical_not(has_after)))(no_after)
    pl.when(jnp.logical_and(core == 1, jnp.logical_not(has_before)))(no_before)

    pl.when(core == 1)(make_picks)
    with jax.named_scope("entry_wait"):
        pl.semaphore_wait(barrier, groups + 1 + 2 * core)

    posts = []
    for distance in order:
        posts.append(
            remote(
                stats.at[me],
                stats.at[me],
                stat_send,
                stat_recv.at[lax.rem(distance + groups, groups)],
                along(distance),
            )
        )
        posts[-1].start()

    with jax.named_scope("raw"):
        pl.when(core == 0)(raw_first)
        pl.when(core == 1)(raw_second)
    with jax.named_scope("stats_wait"):
        for distance in range(1, groups):
            origin = lax.rem(me - distance + groups, groups)
            ref = stats.at[origin]
            pltpu.make_async_copy(ref, ref, stat_recv.at[distance]).wait()
    total = stats[0]
    for group in range(1, groups):
        total = total + stats[group]
    count = jnp.maximum(total[0:lanes], 1.0)
    mean = total[lanes : 2 * lanes] / count
    var = total[2 * lanes : 3 * lanes] / count - mean * mean
    rate = lax.rsqrt(var + 1e-05)
    mean_line = jnp.concatenate([mean[i : i + 1] for i in range(lanes)], axis=1)
    rate_line = jnp.concatenate([rate[i : i + 1] for i in range(lanes)], axis=1)

    def arrived(ref, sem):
        pltpu.make_async_copy(ref, ref, sem).wait()

    def swap(block):
        return remote(
            blocks.at[block],
            blocks.at[block],
            core_send,
            core_recv,
            other,
        )

    def swap_strip(strip):
        cols = pl.ds(strip * 128, 128)
        return remote(
            blocks.at[0, :, cols],
            blocks.at[0, :, cols],
            core_send,
            core_recv,
            other,
        )

    def ahead_copy(chunk):
        return remote(
            blocks.at[0, :, pl.ds(chunk * 128, 128)],
            ahead.at[chunk],
            x_send,
            x_recv.at[0, chunk - 1],
            before_b,
        )

    def behind_copy(chunk):
        return remote(
            ordered.at[:, pl.ds(chunk * 128, 128)],
            behind.at[chunk],
            x_send,
            x_recv.at[1, chunk - 1],
            after_b,
        )

    def standardize(strip):
        cols = slice(strip * 128, strip * 128 + 128)
        mean_row = mean_line[:, cols]
        rate_row = rate_line[:, cols]

        def some_rows(step, carry):
            span = pl.ds(pl.multiple_of(step * 128, 128), 128)
            v = dose_v[span, cols].astype(F32)
            m = seen_v[span, cols].astype(F32)
            blocks[core, span, cols] = (m * (v - mean_row) * rate_row).astype(BF16)
            return carry

        lax.fori_loop(0, rows // 128, some_rows, 0)

    def first_core_sends():
        line_ours[0:1] = mean_line[:, 0:128]
        line_ours[1:2] = rate_line[:, 0:128]
        pl.when(sends_ahead)(lambda: raw_copy(0, 1).start())
        for chunk in range(1, 4):
            standardize(chunk)
            pl.when(sends_ahead)(ahead_copy(chunk).start)
            swap_strip(chunk).start()
        standardize(0)
        swap_strip(0).start()

    def second_core_sends():
        parts = []
        for line in (mean_line, rate_line):
            for _ in range(3):
                top = line.astype(BF16)
                line = line - top.astype(F32)
                parts.append(top)
        parts = jnp.concatenate(parts + [jnp.zeros((10, width), BF16)], axis=0)
        picked = jnp.dot(parts, picks[...], preferred_element_type=F32)
        mean_row = picked[0:1] + picked[1:2] + picked[2:3]
        rate_row = picked[3:4] + picked[4:5] + picked[5:6]
        line_ours[0:1] = mean_row[:, 0:128]
        line_ours[1:2] = rate_row[:, 0:128]
        pl.when(sends_behind)(lambda: raw_copy(1, 1).start())
        for chunk in range(1, 4):
            cols = slice(128 * chunk, 128 * chunk + 128)
            rest = slice(128 * chunk - 128, 128 * chunk)

            def some_rows(step, carry):
                span = pl.ds(pl.multiple_of(step * 128, 128), 128)
                v = raw_rest[0, span, rest].astype(F32)
                m = raw_rest[1, span, rest].astype(F32)
                z = m * (v - mean_row[:, cols]) * rate_row[:, cols]
                ordered[span, cols] = z.astype(BF16)
                return carry

            lax.fori_loop(0, rows // 128, some_rows, 0)
            pl.when(sends_behind)(behind_copy(chunk).start)
        for strip in range(4):
            standardize(strip)
        if CROSS == 0:
            swap(1).start()

    with jax.named_scope("standardize"):
        pl.when(core == 0)(first_core_sends)
        pl.when(core == 1)(second_core_sends)

    early = [
        Chain(
            groups,
            (OWN_STRIDE, CROSS_STRIDE)[number],
            part_e.at[number],
            stage_e.at[number],
            slots_e.at[number],
            e_send.at[number],
            e_recv.at[number],
            along,
        )
        for number in range(2)
    ]
    def end_sem(unit, third, slot):
        if third < 2:
            return l_recv.at[unit, slot]
        return t_recv.at[LATE_ENDS[unit].index(slot) + LATE_FROM[unit]]

    def thirds(unit):
        chunk, first, high, _ = LATE[unit]
        line = pl.ds(first, high)

        def last(slot, distance, source):
            homes = (beside(other, distance), along(distance), beside(before_b, distance))
            return [
                remote(
                    source.at[:, pl.ds(128 * third, 128)],
                    slots_l.at[chunk, slot, line, pl.ds(128 * third, 128)],
                    t_send.at[unit],
                    end_sem(unit, third, slot),
                    homes[third],
                )
                for third in range(3)
            ]

        return last

    late = [
        Chain(
            groups,
            stride,
            part_l.at[chunk, :, pl.ds(first, high)],
            stage_l.at[chunk, :, :, pl.ds(first, high)],
            slots_l.at[chunk, :, pl.ds(first, high)],
            l_send.at[unit],
            l_recv.at[unit],
            along,
            thirds(unit),
        )
        for unit, (chunk, first, high, stride) in enumerate(LATE)
    ]

    def own_term(chunk, third):
        cols = pl.ds(128 * third, 128)
        return remote(
            ours_l.at[chunk, :, cols],
            home_l.at[chunk, :, cols],
            h_send,
            h_recv.at[chunk],
            other if third == 0 else before_b,
        )

    def landed(unit, third):
        chunk, first, high, _ = LATE[unit]
        total = jnp.zeros((high, 128), F32)
        for slot in late[unit].last_slots():
            ref = slots_l.at[
                chunk, slot, pl.ds(first, high), pl.ds(128 * third, 128)
            ]
            arrived(ref, end_sem(unit, third, slot))
            total = total + decode(ref[...])
        return total

    def early_gram(number):
        left, right = (core, core) if number == 0 else (0, 1)
        for strip in range(4):
            cols = slice(strip * 128, strip * 128 + 128)
            product = gram(blocks[left, :, cols], blocks[right])
            part_e[number, strip * 4 : strip * 4 + 4] = product.reshape(4, 32, 512)

    def raw_standardize(side):
        raw = (raw_ahead, raw_behind)[side]
        line = (line_ahead, line_behind)[side]
        target = (ahead, behind)[side]
        with jax.named_scope("raw_wait"):
            arrived(raw, r_recv.at[side, 0])
            arrived(line, r_recv.at[side, 1])
        mean_row = line[0:1]
        rate_row = line[1:2]

        def some_rows(step, carry):
            span = pl.ds(pl.multiple_of(step * 128, 128), 128)
            v = raw[0, span].astype(F32)
            m = raw[1, span].astype(F32)
            target[0, span] = (m * (v - mean_row) * rate_row).astype(BF16)
            return carry

        lax.fori_loop(0, rows // 128, some_rows, 0)

    def late_gram(chunk):
        if chunk == 0:
            pl.when(has_after)(lambda: raw_standardize(0))
            pl.when(has_before)(lambda: raw_standardize(1))
        else:
            with jax.named_scope("ahead_wait"):
                pl.when(has_after)(
                    lambda: arrived(ahead.at[chunk], x_recv.at[0, chunk - 1])
                )
            with jax.named_scope("behind_wait"):
                pl.when(has_before)(
                    lambda: arrived(behind.at[chunk], x_recv.at[1, chunk - 1])
                )
        with jax.named_scope("late_gram"):
            part = part_l.at[chunk]
            for block in range(2):
                product = gram(blocks[block], ahead[chunk])
                cols = slice(block * 128, block * 128 + 128)
                part[:, :, cols] = product.reshape(16, 32, 128)
            product = gram(behind[chunk], blocks[1])
            for piece in range(4):
                cols = slice(piece * 128, piece * 128 + 128)
                part[:, piece * 8 : piece * 8 + 8, 256:384] = product[:, cols].reshape(
                    16, 8, 128
                )
            ours_l[chunk] = encode(part[me])
            own_term(chunk, 0).start()
            own_term(chunk, 2).start()

    scale = 1.0 / samples

    def early_copy():
        return remote(give_e, take_e, f_send.at[0], f_recv.at[0], other)

    def end(number):
        if number == 0:
            out[:, 0:512] = early[0].finish() * scale
        elif number == 1:
            total = early[1].finish() * scale
            if CROSS == 0:
                out[:, 512:1024] = total
            else:
                give_e[...] = total
                early_copy().start()
        else:
            unit = number - 2
            chunk, first, high, _ = LATE[unit]
            line = slice(first, first + high)
            total = landed(unit, 1) + part_l[chunk, me, line, 128:256]
            cols = slice(512 + 128 * chunk, 640 + 128 * chunk)
            out[line, cols] = total * scale

    def end_first(unit):
        chunk, first, high, _ = LATE[unit]
        line = slice(first, first + high)
        if unit == 0 or LATE[unit - 1][0] != chunk:
            arrived(home_l.at[chunk, :, pl.ds(0, 128)], h_recv.at[chunk])
        total = landed(unit, 0) + decode(home_l[chunk, line, 0:128])
        cols = slice(1024 + 128 * chunk, 1152 + 128 * chunk)
        out[line, cols] = total * scale

    def end_second(unit):
        chunk, first, high, _ = LATE[unit]
        line = slice(first, first + high)
        if unit == 0 or LATE[unit - 1][0] != chunk:
            arrived(home_l.at[chunk, :, pl.ds(256, 128)], h_recv.at[chunk])
        total = landed(unit, 2) + decode(home_l[chunk, line, 256:384])
        value = total * scale
        for piece in range(high // 8):
            cols = 1024 + 128 * (first // 8 + piece)
            out[8 * chunk : 8 * chunk + 8, cols : cols + 128] = value[
                piece * 8 : piece * 8 + 8
            ]

    def run(side):
        units = early + late
        swapped = False
        for number, index in ORDER[side]:
            name = ("own", "cross")[number] if number < 2 else f"late{number - 2}"
            steps = units[number].levels()
            if number > 0 and not swapped:
                swapped = True
                if side == 1 or CROSS == 0:
                    with jax.named_scope("swap_wait"):
                        swap(1 - side).wait_recv()
            if index == 0:
                with jax.named_scope(name + "_gram"):
                    if number < 2:
                        early_gram(number)
                    elif number == 2 or LATE[number - 3][0] != LATE[number - 2][0]:
                        late_gram(LATE[number - 2][0])
            with jax.named_scope(f"{name}_{index}"):
                if index < len(steps):
                    for way, offset in steps[index]:
                        units[number].visit(way, offset)
                else:
                    end(number)

    def exchange_sent(side):
        arrived(ahead.at[pl.ds(0, 3)], x_send)
        for number in range(2):
            raw_copy(side, number).wait_send()

    def first_core():
        run(0)
        with jax.named_scope("ends"):
            for unit in range(len(LATE)):
                end_first(unit)
            if CROSS == 1:
                arrived(take_e, f_recv.at[0])
                out[:, 512:1024] = take_e[...]
        swap(0).wait_send()
        for chain in early[: 2 - CROSS]:
            chain.drain()
        pl.when(has_before)(lambda: exchange_sent(0))

    def second_core():
        run(1)
        with jax.named_scope("ends"):
            for unit in range(len(LATE)):
                end_second(unit)
        for chain in early[: 1 + CROSS]:
            chain.drain()
        for unit, chain in enumerate(late):
            chain.drain(t_send.at[unit])
        if CROSS == 1:
            early_copy().wait_send()
        else:
            swap(1).wait_send()
        pl.when(has_after)(lambda: exchange_sent(1))
        arrived(ours_l.at[:, :, pl.ds(0, 256)], h_send)

    pl.when(core == 0)(first_core)
    pl.when(core == 1)(second_core)

    sent = stats.at[pl.ds(0, groups - 1)]
    pltpu.make_async_copy(sent, sent, stat_send).wait()


def solution(mesh):
    groups, snps = mesh.shape["samp"], mesh.shape["snp"]

    def local(dosages, observed):
        rows, width = dosages.shape
        vmem = pltpu.VMEM
        dma = pltpu.SemaphoreType.DMA
        return pl.pallas_call(
            functools.partial(band_kernel, groups, snps // 2),
            out_shape=jax.ShapeDtypeStruct((width // groups, 3 * width), F32),
            in_specs=[pl.BlockSpec(memory_space=pl.ANY)] * 2,
            out_specs=pl.BlockSpec(memory_space=pltpu.VMEM),
            scratch_shapes=[
                vmem((rows, width), BF16),
                vmem((rows, width), jnp.int32),
                vmem((groups, 12, 128), F32),
                vmem((2, rows, width), BF16),
                vmem((width, width), BF16),
                vmem((rows, width), BF16),
                vmem((4, rows, 128), BF16),
                vmem((4, rows, 128), BF16),
                vmem((2, rows, 128), BF16),
                vmem((2, rows, 384), BF16),
                vmem((2, rows, 128), BF16),
                vmem((2, rows, 128), BF16),
                vmem((8, 128), F32),
                vmem((8, 128), F32),
                vmem((8, 128), F32),
                vmem((2, groups, 32, 512), F32),
                vmem((4, groups, 32, 384), F32),
                vmem((2, 2, 8, 32, 512), jnp.int16),
                vmem((4, 2, 8, 32, 384), jnp.int16),
                vmem((2, 15, 32, 512), jnp.int16),
                vmem((4, 15, 32, 384), jnp.int16),
                vmem((4, 32, 384), jnp.int16),
                vmem((4, 32, 384), jnp.int16),
                vmem((32, 512), F32),
                vmem((32, 512), F32),
                dma((2, 4)),
                dma,
                dma((groups,)),
                dma,
                dma,
                dma,
                dma((2, 3)),
                dma((2,)),
                dma((2, 2)),
                dma((2,)),
                dma((2, 15)),
                dma((len(LATE),)),
                dma((len(LATE), 15)),
                dma((len(LATE),)),
                dma((LATE_FROM[-1],)),
                dma,
                dma((4,)),
                dma((1,)),
                dma((1,)),
            ],
            compiler_params=pltpu.CompilerParams(
                collective_id=0,
                has_side_effects=True,
                vmem_limit_bytes=56 * 2**20,
            ),
            cost_estimate=pl.CostEstimate(
                flops=2 * 3 * rows * width * width,
                bytes_accessed=6 * rows * width,
                transcendentals=0,
            ),
            name="band",
        )(dosages, observed)

    return jax.shard_map(
        local,
        mesh=mesh,
        in_specs=(P("samp", "snp"), P("samp", "snp")),
        out_specs=P(("snp", "samp"), None),
        check_vma=False,
    )
```

```python
import functools
import math

import jax
import jax.numpy as jnp
from jax import lax
from jax.experimental import pallas as pl
from jax.experimental.pallas import tpu as pltpu
from jax.sharding import PartitionSpec as P

MESH = pl.DeviceIdType.MESH
F32 = jnp.float32
BF16 = jnp.bfloat16

STEPS = 1650.0
FINE = 4096.0


OWN_STRIDE = 1
CROSS = 1
CROSS_STRIDE = 1
LATE = ((0, 0, 32, 1), (1, 0, 32, 1), (2, 0, 32, 2), (3, 0, 32, 2))
ORDER = (
    ((0, 0), (0, 1), (0, 2), (0, 3), (0, 4), (0, 5), (0, 6), (0, 7), (0, 8),),
    ((0, 0), (1, 0), (0, 1), (2, 0), (3, 0), (0, 2), (1, 1), (2, 1), (3, 1), (0, 3), (1, 2), (4, 0), (2, 2), (3, 2), (0, 4), (1, 3), (5, 0), (3, 3), (2, 3), (0, 5), (4, 1), (1, 4), (3, 4), (2, 4), (0, 6), (1, 5), (5, 1), (4, 2), (3, 5), (2, 5), (0, 7), (1, 6), (5, 2), (3, 6), (2, 6), (4, 3), (0, 8), (1, 7), (3, 7), (2, 7), (5, 3), (1, 8), (4, 4), (3, 8), (2, 8), (5, 4),),
)


def encode(x):
    q = jnp.minimum(STEPS * jnp.log(1.0 + FINE * jnp.abs(x)) + 0.5, 32767.0).astype(
        jnp.int32
    )
    return jnp.where(x < 0.0, -q, q).astype(jnp.int16)


def decode(q):
    f = q.astype(jnp.int32).astype(F32)
    a = (jnp.exp(jnp.abs(f) * (1.0 / STEPS)) - 1.0) * (1.0 / FINE)
    return jnp.where(f < 0.0, -a, a)


def gram(left, right):
    return lax.dot_general(
        left, right, (((0,), (0,)), ((), ())), preferred_element_type=F32
    )


class Chain:
    def __init__(self, groups, stride, part, stage, slots, send, recv, device, last=None):
        self.groups = groups
        self.reach = (groups // 2, groups - 1 - groups // 2)
        self.stride = tuple(min(stride, reach) for reach in self.reach)
        self.part, self.stage, self.slots = part, stage, slots
        self.send, self.recv, self.device, self.last = send, recv, device, last

    def slot(self, way, number):
        return way * self.reach[0] + number - 1

    def hops(self, way, offset, source):
        stride, reach = self.stride[way], self.reach[way]
        sign = 1 if way == 0 else -1
        slot = offset - stride if offset > stride else reach - stride + offset
        slot = self.slot(way, slot)
        if offset > stride or self.last is None:
            return [
                pltpu.make_async_remote_copy(
                    src_ref=source,
                    dst_ref=self.slots.at[slot],
                    send_sem=self.send,
                    recv_sem=self.recv.at[slot],
                    device_id=self.device(sign * min(stride, offset)),
                    device_id_type=MESH,
                )
            ]
        return self.last(slot, sign * offset, source)

    def arrival(self, way, number):
        slot = self.slot(way, number)
        ref = self.slots.at[slot]
        return pltpu.make_async_copy(ref, ref, self.recv.at[slot])

    def own(self, way, offset):
        me = lax.axis_index("samp")
        sign = 1 if way == 0 else -1
        return lax.rem(me + sign * offset + self.groups, self.groups)

    def source(self, way, offset):
        reach, stride = self.reach[way], self.stride[way]
        if offset + stride > reach:
            return self.stage.at[way, reach - offset]
        return self.slots.at[self.slot(way, offset)]

    def last_slots(self):
        return [
            self.slot(way, self.reach[way] - self.stride[way] + near)
            for near in range(1, max(self.stride) + 1)
            for way in (0, 1)
            if near <= self.stride[way]
        ]

    def visit(self, way, offset):
        reach, stride = self.reach[way], self.stride[way]
        ref = self.source(way, offset)
        total = self.part[self.own(way, offset)]
        if offset + stride <= reach:
            self.arrival(way, offset).wait()
            total = total + decode(ref[...])
        ref[...] = encode(total)
        for copy in self.hops(way, offset, ref):
            copy.start()

    def levels(self):
        steps = []
        for way in (0, 1):
            for place, offset in enumerate(range(self.reach[way], 0, -1)):
                number = place // self.stride[way]
                if number == len(steps):
                    steps.append([])
                steps[number].append((place, way, offset))
        return [[visit[1:] for visit in sorted(step)] for step in steps]

    def finish(self):
        total = self.part[lax.axis_index("samp")]
        for slot in self.last_slots():
            ref = self.slots.at[slot]
            pltpu.make_async_copy(ref, ref, self.recv.at[slot]).wait()
            total = total + decode(ref[...])
        return total

    def drain(self, last_send=None):
        whole, end = sum(self.reach), sum(self.stride)
        if last_send is not None:
            ref = self.slots.at[pl.ds(0, end)]
            pltpu.make_async_copy(ref, ref, last_send).wait()
            whole -= end
        if whole:
            ref = self.slots.at[pl.ds(0, whole)]
            pltpu.make_async_copy(ref, ref, self.send).wait()


LATE_ENDS = [
    Chain(16, unit[3], None, None, None, None, None, None).last_slots() for unit in LATE
]
LATE_FROM = [sum(len(e) for e in LATE_ENDS[:n]) for n in range(len(LATE) + 1)]


def band_kernel(
    groups,
    chips,
    dosages,
    observed,
    out,
    dose_v,
    seen_v,
    stats,
    blocks,
    picks,
    ordered,
    ahead,
    behind,
    raw_ours,
    raw_rest,
    raw_ahead,
    raw_behind,
    line_ours,
    line_ahead,
    line_behind,
    part_e,
    part_l,
    stage_e,
    stage_l,
    slots_e,
    slots_l,
    ours_l,
    home_l,
    give_e,
    take_e,
    load_sem,
    stat_send,
    stat_recv,
    core_send,
    core_recv,
    x_send,
    x_recv,
    r_send,
    r_recv,
    e_send,
    e_recv,
    l_send,
    l_recv,
    t_send,
    t_recv,
    h_send,
    h_recv,
    f_send,
    f_recv,
):
    snp, me = lax.axis_index("snp"), lax.axis_index("samp")
    core = lax.rem(snp, 2)
    chip = lax.div(snp, 2)
    rows, width = dose_v.shape
    samples = rows * groups
    count_snp = 2 * chips

    def along(distance):
        return (snp, lax.rem(me + distance + groups, groups))

    other = (snp + 1 - 2 * core, me)
    before_b = (lax.rem(2 * chip + count_snp - 1, count_snp), me)
    after_b = (lax.rem(2 * chip + 3, count_snp), me)
    after_a = (lax.rem(2 * chip + 2, count_snp), me)

    has_before, has_after = chip > 0, chip < chips - 1
    sends_ahead = jnp.logical_and(core == 0, has_before)
    sends_behind = jnp.logical_and(core == 1, has_after)

    def remote(src, dst, send, recv, device):
        return pltpu.make_async_remote_copy(
            src_ref=src,
            dst_ref=dst,
            send_sem=send,
            recv_sem=recv,
            device_id=device,
            device_id_type=MESH,
        )

    half = groups // 2
    order = [half] + [sign * d for d in range(half - 1, 0, -1) for sign in (1, -1)]
    barrier = pltpu.get_barrier_semaphore()

    def greet(peers):
        for peer in peers:
            pl.semaphore_signal(barrier, inc=1, device_id=peer, device_id_type=MESH)

    def beside(device, distance):
        return (device[0], lax.rem(me + distance + groups, groups))

    greet([along(d) for d in order] + [other, before_b])
    pl.when(core == 1)(lambda: greet([after_a, after_b]))

    pieces = load_sem.shape[1]
    high = rows // pieces

    def load(piece):
        span = pl.ds(piece * high, high)
        return (
            pltpu.make_async_copy(
                dosages.at[span], dose_v.at[span], load_sem.at[0, piece]
            ),
            pltpu.make_async_copy(
                observed.at[span], seen_v.at[span], load_sem.at[1, piece]
            ),
        )


    for piece in range(pieces):
        for copy in load(piece):
            copy.start()

    def make_picks():
        line = lax.broadcasted_iota(jnp.int32, (width, width), 0)
        col = lax.broadcasted_iota(jnp.int32, (width, width), 1)
        from_row = 32 * ((col >> 3) & 15) + 8 * (col >> 7) + (col & 7)
        picks[...] = jnp.where(line == from_row, 1.0, 0.0).astype(BF16)

    def add_rows(step, carry):
        span = pl.ds(pl.multiple_of(step * 32, 32), 32)
        v = dose_v[span].astype(F32)
        m = seen_v[span].astype(F32)
        mv = m * v
        sums = []
        for acc, term in zip(carry, (m, mv, mv * v)):
            sums.append(acc + jnp.sum(term.reshape(4, 8, width), axis=0))
        return tuple(sums)

    carry = tuple(jnp.zeros((8, width), F32) for _ in range(3))
    for piece in range(pieces):
        for copy in load(piece):
            copy.wait()
        carry = lax.fori_loop(
            piece * high // 32, (piece + 1) * high // 32, add_rows, carry
        )
    lanes = width // 128
    for kind, acc in enumerate(carry):
        line = jnp.sum(acc, axis=0, keepdims=True)
        for lane in range(lanes):
            row = kind * lanes + lane
            stats[me, row : row + 1, :] = line[:, lane * 128 : lane * 128 + 128]

    def raw_first():
        raw_ours[0] = dose_v[:, 0:128]
        raw_ours[1] = seen_v[:, 0:128].astype(F32).astype(BF16)
        pl.when(has_before)(raw_copy(0, 0).start)

    def raw_second():
        ordered[...] = seen_v[...].astype(F32).astype(BF16)
        first = picks[:, 0:128]
        raw_ours[0] = jnp.dot(
            dose_v[...], first, preferred_element_type=F32
        ).astype(BF16)
        raw_ours[1] = jnp.dot(
            ordered[...], first, preferred_element_type=F32
        ).astype(BF16)
        pl.when(has_after)(raw_copy(1, 0).start)
        for pair in (slice(128, 256), slice(256, 512)):
            cols = slice(pair.start - 128, pair.stop - 128)
            raw_rest[0, :, cols] = jnp.dot(
                dose_v[...], picks[:, pair], preferred_element_type=F32
            ).astype(BF16)
            raw_rest[1, :, cols] = jnp.dot(
                ordered[...], picks[:, pair], preferred_element_type=F32
            ).astype(BF16)

    def raw_copy(side, number):
        return remote(
            (raw_ours, line_ours)[number],
            ((raw_ahead, raw_behind), (line_ahead, line_behind))[number][side],
            r_send.at[number],
            r_recv.at[side, number],
            (before_b, after_b)[side],
        )

    def no_after():
        ahead[...] = jnp.zeros(ahead.shape, BF16)

    def no_before():
        behind[...] = jnp.zeros(behind.shape, BF16)

    pl.when(jnp.logical_and(core == 1, jnp.logical_not(has_after)))(no_after)
    pl.when(jnp.logical_and(core == 1, jnp.logical_not(has_before)))(no_before)

    pl.when(core == 1)(make_picks)
    with jax.named_scope("entry_wait"):
        pl.semaphore_wait(barrier, groups + 1 + 2 * core)

    posts = []
    for distance in order:
        posts.append(
            remote(
                stats.at[me],
                stats.at[me],
                stat_send,
                stat_recv.at[lax.rem(distance + groups, groups)],
                along(distance),
            )
        )
        posts[-1].start()

    with jax.named_scope("raw"):
        pl.when(core == 0)(raw_first)
        pl.when(core == 1)(raw_second)
    with jax.named_scope("stats_wait"):
        for distance in range(1, groups):
            origin = lax.rem(me - distance + groups, groups)
            ref = stats.at[origin]
            pltpu.make_async_copy(ref, ref, stat_recv.at[distance]).wait()
    total = stats[0]
    for group in range(1, groups):
        total = total + stats[group]
    count = jnp.maximum(total[0:lanes], 1.0)
    mean = total[lanes : 2 * lanes] / count
    var = total[2 * lanes : 3 * lanes] / count - mean * mean
    rate = lax.rsqrt(var + 1e-05)
    mean_line = jnp.concatenate([mean[i : i + 1] for i in range(lanes)], axis=1)
    rate_line = jnp.concatenate([rate[i : i + 1] for i in range(lanes)], axis=1)

    def arrived(ref, sem):
        pltpu.make_async_copy(ref, ref, sem).wait()

    def swap(block):
        return remote(
            blocks.at[block],
            blocks.at[block],
            core_send,
            core_recv,
            other,
        )

    def swap_strip(strip):
        cols = pl.ds(strip * 128, 128)
        return remote(
            blocks.at[0, :, cols],
            blocks.at[0, :, cols],
            core_send,
            core_recv,
            other,
        )

    def ahead_copy(chunk):
        return remote(
            blocks.at[0, :, pl.ds(chunk * 128, 128)],
            ahead.at[chunk],
            x_send,
            x_recv.at[0, chunk - 1],
            before_b,
        )

    def behind_copy(chunk):
        return remote(
            ordered.at[:, pl.ds(chunk * 128, 128)],
            behind.at[chunk],
            x_send,
            x_recv.at[1, chunk - 1],
            after_b,
        )

    def standardize(strip):
        cols = slice(strip * 128, strip * 128 + 128)
        mean_row = mean_line[:, cols]
        rate_row = rate_line[:, cols]

        def some_rows(step, carry):
            span = pl.ds(pl.multiple_of(step * 128, 128), 128)
            v = dose_v[span, cols].astype(F32)
            m = seen_v[span, cols].astype(F32)
            blocks[core, span, cols] = (m * (v - mean_row) * rate_row).astype(BF16)
            return carry

        lax.fori_loop(0, rows // 128, some_rows, 0)

    def first_core_sends():
        line_ours[0:1] = mean_line[:, 0:128]
        line_ours[1:2] = rate_line[:, 0:128]
        pl.when(sends_ahead)(lambda: raw_copy(0, 1).start())
        for chunk in range(1, 4):
            standardize(chunk)
            pl.when(sends_ahead)(ahead_copy(chunk).start)
            swap_strip(chunk).start()
        standardize(0)
        swap_strip(0).start()

    def second_core_sends():
        parts = []
        for line in (mean_line, rate_line):
            for _ in range(3):
                top = line.astype(BF16)
                line = line - top.astype(F32)
                parts.append(top)
        parts = jnp.concatenate(parts + [jnp.zeros((10, width), BF16)], axis=0)
        picked = jnp.dot(parts, picks[...], preferred_element_type=F32)
        mean_row = picked[0:1] + picked[1:2] + picked[2:3]
        rate_row = picked[3:4] + picked[4:5] + picked[5:6]
        line_ours[0:1] = mean_row[:, 0:128]
        line_ours[1:2] = rate_row[:, 0:128]
        pl.when(sends_behind)(lambda: raw_copy(1, 1).start())
        for chunk in range(1, 4):
            cols = slice(128 * chunk, 128 * chunk + 128)
            rest = slice(128 * chunk - 128, 128 * chunk)

            def some_rows(step, carry):
                span = pl.ds(pl.multiple_of(step * 128, 128), 128)
                v = raw_rest[0, span, rest].astype(F32)
                m = raw_rest[1, span, rest].astype(F32)
                z = m * (v - mean_row[:, cols]) * rate_row[:, cols]
                ordered[span, cols] = z.astype(BF16)
                return carry

            lax.fori_loop(0, rows // 128, some_rows, 0)
            pl.when(sends_behind)(behind_copy(chunk).start)
        for strip in range(4):
            standardize(strip)
        if CROSS == 0:
            swap(1).start()

    with jax.named_scope("standardize"):
        pl.when(core == 0)(first_core_sends)
        pl.when(core == 1)(second_core_sends)

    early = [
        Chain(
            groups,
            (OWN_STRIDE, CROSS_STRIDE)[number],
            part_e.at[number],
            stage_e.at[number],
            slots_e.at[number],
            e_send.at[number],
            e_recv.at[number],
            along,
        )
        for number in range(2)
    ]
    def end_sem(unit, third, slot):
        if third < 2:
            return l_recv.at[unit, slot]
        return t_recv.at[LATE_ENDS[unit].index(slot) + LATE_FROM[unit]]

    def thirds(unit):
        chunk, first, high, _ = LATE[unit]
        line = pl.ds(first, high)

        def last(slot, distance, source):
            homes = (beside(other, distance), along(distance), beside(before_b, distance))
            return [
                remote(
                    source.at[:, pl.ds(128 * third, 128)],
                    slots_l.at[chunk, slot, line, pl.ds(128 * third, 128)],
                    t_send.at[unit],
                    end_sem(unit, third, slot),
                    homes[third],
                )
                for third in range(3)
            ]

        return last

    late = [
        Chain(
            groups,
            stride,
            part_l.at[chunk, :, pl.ds(first, high)],
            stage_l.at[chunk, :, :, pl.ds(first, high)],
            slots_l.at[chunk, :, pl.ds(first, high)],
            l_send.at[unit],
            l_recv.at[unit],
            along,
            thirds(unit),
        )
        for unit, (chunk, first, high, stride) in enumerate(LATE)
    ]

    def own_term(chunk, third):
        cols = pl.ds(128 * third, 128)
        return remote(
            ours_l.at[chunk, :, cols],
            home_l.at[chunk, :, cols],
            h_send,
            h_recv.at[chunk],
            other if third == 0 else before_b,
        )

    def landed(unit, third):
        chunk, first, high, _ = LATE[unit]
        total = jnp.zeros((high, 128), F32)
        for slot in late[unit].last_slots():
            ref = slots_l.at[
                chunk, slot, pl.ds(first, high), pl.ds(128 * third, 128)
            ]
            arrived(ref, end_sem(unit, third, slot))
            total = total + decode(ref[...])
        return total

    def early_gram(number):
        left, right = (core, core) if number == 0 else (0, 1)
        for strip in range(4):
            cols = slice(strip * 128, strip * 128 + 128)
            product = gram(blocks[left, :, cols], blocks[right])
            part_e[number, strip * 4 : strip * 4 + 4] = product.reshape(4, 32, 512)

    def raw_standardize(side):
        raw = (raw_ahead, raw_behind)[side]
        line = (line_ahead, line_behind)[side]
        target = (ahead, behind)[side]
        with jax.named_scope("raw_wait"):
            arrived(raw, r_recv.at[side, 0])
            arrived(line, r_recv.at[side, 1])
        mean_row = line[0:1]
        rate_row = line[1:2]

        def some_rows(step, carry):
            span = pl.ds(pl.multiple_of(step * 128, 128), 128)
            v = raw[0, span].astype(F32)
            m = raw[1, span].astype(F32)
            target[0, span] = (m * (v - mean_row) * rate_row).astype(BF16)
            return carry

        lax.fori_loop(0, rows // 128, some_rows, 0)

    def late_gram(chunk):
        if chunk == 0:
            pl.when(has_after)(lambda: raw_standardize(0))
            pl.when(has_before)(lambda: raw_standardize(1))
        else:
            with jax.named_scope("ahead_wait"):
                pl.when(has_after)(
                    lambda: arrived(ahead.at[chunk], x_recv.at[0, chunk - 1])
                )
            with jax.named_scope("behind_wait"):
                pl.when(has_before)(
                    lambda: arrived(behind.at[chunk], x_recv.at[1, chunk - 1])
                )
        with jax.named_scope("late_gram"):
            part = part_l.at[chunk]
            for block in range(2):
                product = gram(blocks[block], ahead[chunk])
                cols = slice(block * 128, block * 128 + 128)
                part[:, :, cols] = product.reshape(16, 32, 128)
            product = gram(behind[chunk], blocks[1])
            for piece in range(4):
                cols = slice(piece * 128, piece * 128 + 128)
                part[:, piece * 8 : piece * 8 + 8, 256:384] = product[:, cols].reshape(
                    16, 8, 128
                )
            ours_l[chunk] = encode(part[me])
            own_term(chunk, 0).start()
            own_term(chunk, 2).start()

    scale = 1.0 / samples

    def early_copy():
        return remote(give_e, take_e, f_send.at[0], f_recv.at[0], other)

    def end(number):
        if number == 0:
            out[:, 0:512] = early[0].finish() * scale
        elif number == 1:
            total = early[1].finish() * scale
            if CROSS == 0:
                out[:, 512:1024] = total
            else:
                give_e[...] = total
                early_copy().start()
        else:
            unit = number - 2
            chunk, first, high, _ = LATE[unit]
            line = slice(first, first + high)
            total = landed(unit, 1) + part_l[chunk, me, line, 128:256]
            cols = slice(512 + 128 * chunk, 640 + 128 * chunk)
            out[line, cols] = total * scale

    def end_first(unit):
        chunk, first, high, _ = LATE[unit]
        line = slice(first, first + high)
        if unit == 0 or LATE[unit - 1][0] != chunk:
            arrived(home_l.at[chunk, :, pl.ds(0, 128)], h_recv.at[chunk])
        total = landed(unit, 0) + decode(home_l[chunk, line, 0:128])
        cols = slice(1024 + 128 * chunk, 1152 + 128 * chunk)
        out[line, cols] = total * scale

    def end_second(unit):
        chunk, first, high, _ = LATE[unit]
        line = slice(first, first + high)
        if unit == 0 or LATE[unit - 1][0] != chunk:
            arrived(home_l.at[chunk, :, pl.ds(256, 128)], h_recv.at[chunk])
        total = landed(unit, 2) + decode(home_l[chunk, line, 256:384])
        value = total * scale
        for piece in range(high // 8):
            cols = 1024 + 128 * (first // 8 + piece)
            out[8 * chunk : 8 * chunk + 8, cols : cols + 128] = value[
                piece * 8 : piece * 8 + 8
            ]

    def run(side):
        units = early + late
        swapped = False
        for number, index in ORDER[side]:
            name = ("own", "cross")[number] if number < 2 else f"late{number - 2}"
            steps = units[number].levels()
            if number > 0 and not swapped:
                swapped = True
                if side == 1 or CROSS == 0:
                    with jax.named_scope("swap_wait"):
                        swap(1 - side).wait_recv()
            if index == 0:
                with jax.named_scope(name + "_gram"):
                    if number < 2:
                        early_gram(number)
                    elif number == 2 or LATE[number - 3][0] != LATE[number - 2][0]:
                        late_gram(LATE[number - 2][0])
            with jax.named_scope(f"{name}_{index}"):
                if index < len(steps):
                    for way, offset in steps[index]:
                        units[number].visit(way, offset)
                else:
                    end(number)

    def exchange_sent(side):
        arrived(ahead.at[pl.ds(0, 3)], x_send)
        for number in range(2):
            raw_copy(side, number).wait_send()

    def first_core():
        run(0)
        with jax.named_scope("ends"):
            for unit in range(len(LATE)):
                end_first(unit)
            if CROSS == 1:
                arrived(take_e, f_recv.at[0])
                out[:, 512:1024] = take_e[...]
        swap(0).wait_send()
        for chain in early[: 2 - CROSS]:
            chain.drain()
        pl.when(has_before)(lambda: exchange_sent(0))

    def second_core():
        run(1)
        with jax.named_scope("ends"):
            for unit in range(len(LATE)):
                end_second(unit)
        for chain in early[: 1 + CROSS]:
            chain.drain()
        for unit, chain in enumerate(late):
            chain.drain(t_send.at[unit])
        if CROSS == 1:
            early_copy().wait_send()
        else:
            swap(1).wait_send()
        pl.when(has_after)(lambda: exchange_sent(1))
        arrived(ours_l.at[:, :, pl.ds(0, 256)], h_send)

    pl.when(core == 0)(first_core)
    pl.when(core == 1)(second_core)

    sent = stats.at[pl.ds(0, groups - 1)]
    pltpu.make_async_copy(sent, sent, stat_send).wait()


def solution(mesh):
    groups, snps = mesh.shape["samp"], mesh.shape["snp"]

    def local(dosages, observed):
        rows, width = dosages.shape
        vmem = pltpu.VMEM
        dma = pltpu.SemaphoreType.DMA
        return pl.pallas_call(
            functools.partial(band_kernel, groups, snps // 2),
            out_shape=jax.ShapeDtypeStruct((width // groups, 3 * width), F32),
            in_specs=[pl.BlockSpec(memory_space=pl.ANY)] * 2,
            out_specs=pl.BlockSpec(memory_space=pltpu.VMEM),
            scratch_shapes=[
                vmem((rows, width), BF16),
                vmem((rows, width), jnp.int32),
                vmem((groups, 12, 128), F32),
                vmem((2, rows, width), BF16),
                vmem((width, width), BF16),
                vmem((rows, width), BF16),
                vmem((4, rows, 128), BF16),
                vmem((4, rows, 128), BF16),
                vmem((2, rows, 128), BF16),
                vmem((2, rows, 384), BF16),
                vmem((2, rows, 128), BF16),
                vmem((2, rows, 128), BF16),
                vmem((8, 128), F32),
                vmem((8, 128), F32),
                vmem((8, 128), F32),
                vmem((2, groups, 32, 512), F32),
                vmem((4, groups, 32, 384), F32),
                vmem((2, 2, 8, 32, 512), jnp.int16),
                vmem((4, 2, 8, 32, 384), jnp.int16),
                vmem((2, 15, 32, 512), jnp.int16),
                vmem((4, 15, 32, 384), jnp.int16),
                vmem((4, 32, 384), jnp.int16),
                vmem((4, 32, 384), jnp.int16),
                vmem((32, 512), F32),
                vmem((32, 512), F32),
                dma((2, 4)),
                dma,
                dma((groups,)),
                dma,
                dma,
                dma,
                dma((2, 3)),
                dma((2,)),
                dma((2, 2)),
                dma((2,)),
                dma((2, 15)),
                dma((len(LATE),)),
                dma((len(LATE), 15)),
                dma((len(LATE),)),
                dma((LATE_FROM[-1],)),
                dma,
                dma((4,)),
                dma((1,)),
                dma((1,)),
            ],
            compiler_params=pltpu.CompilerParams(
                collective_id=0,
                has_side_effects=True,
                vmem_limit_bytes=56 * 2**20,
            ),
            cost_estimate=pl.CostEstimate(
                flops=2 * 3 * rows * width * width,
                bytes_accessed=6 * rows * width,
                transcendentals=0,
            ),
            name="band",
        )(dosages, observed)

    return jax.shard_map(
        local,
        mesh=mesh,
        in_specs=(P("samp", "snp"), P("samp", "snp")),
        out_specs=P(("snp", "samp"), None),
        check_vma=False,
    )
```
